128 devices in a mesh: dp: 16 (over y, x), expert: 8 (over z, core).
Axes of the slice: x: 4, y: 4, z: 4, core: 2. Of those that a mesh axis runs over, the one named last changes fastest.
Arguments:
- tokens: bfloat16 [16384, 4096], P(('dp', 'expert')), may hold values from -6 to 6
- cotangent: bfloat16 [16384, 4096], P(('dp', 'expert')), may hold values from -6 to 6
- chosen: int32 [128, 8, 4], P(('dp', 'expert')), may hold values from 0 to 127, as said below
- counts: int32 [128, 8], P(('dp', 'expert')), may hold values from 0 to 4, as said below
- gate_prob: bfloat16 [128, 8, 4], P(('dp', 'expert')), may hold values from 0.049804688 to 1
- w_gate: bfloat16 [8, 4096, 7168], P('expert', None, 'dp'), may hold values from -0.09375 to 0.09375
- w_up: bfloat16 [8, 4096, 7168], P('expert', None, 'dp'), may hold values from -0.09375 to 0.09375
- w_down: bfloat16 [8, 7168, 4096], P('expert', 'dp'), may hold values from -0.0625 to 0.0625
Outputs:
- combined: bfloat16 [16384, 4096], P(('dp', 'expert'))
- token_grad: bfloat16 [16384, 4096], P(('dp', 'expert'))
- prob_grad: bfloat16 [128, 8, 4], P(('dp', 'expert'))
- grad_gate: bfloat16 [8, 4096, 7168], P('expert', None, 'dp')
- grad_up: bfloat16 [8, 4096, 7168], P('expert', None, 'dp')
- grad_down: bfloat16 [8, 7168, 4096], P('expert', 'dp')
The draws below stay inside these ranges and needn't reach their ends.
Inputs may be any that keep to these rules, and one draw needn't show every extreme that they name: The 4 entries of chosen[s, e] are distinct local token indices of shard s; only the first counts[s, e] are used. For every expert, counts over all 128 token shards sum to exactly 256; some shards give 4 tokens to an expert.
All inputs are finite; a program needn't handle non-finite values.
Results may differ from the reference program's by a relative error of at most 0.012.
Values may be sent and summed in bfloat16 or wider, within the bound.
A program may use at most 128 MiB of HBM per device.

```python
import jax
import jax.numpy as jnp
from jax import lax

D = 4096
FF = 7168
M = 4
TOK_DEV = 128
SOURCES = 128
TOKENS = 16384
EXPERTS = 8


def draw_chosen(key, part):
    key = jax.random.fold_in(key, 11)
    subkeys = jax.random.split(key, SOURCES * EXPERTS)

    def pick_row(subkey):
        return jax.random.permutation(subkey, TOK_DEV)[:M]
    picked = jax.vmap(pick_row)(subkeys)
    return picked.reshape(SOURCES, EXPERTS, M).astype(jnp.int32)


def draw_counts(key, part):
    key = jax.random.fold_in(key, 23)
    shard_iota = jnp.arange(SOURCES, dtype=jnp.int32)
    pattern = jnp.where(shard_iota < SOURCES // 4, M, jnp.where(shard_iota < 3 * (SOURCES // 4), M // 2, 0)).astype(jnp.int32)
    subkeys = jax.random.split(key, EXPERTS)

    def spread_col(subkey):
        return pattern[jax.random.permutation(subkey, SOURCES)]
    columns = jax.vmap(spread_col)(subkeys)
    return columns.T.astype(jnp.int32)


def steps_of(own_key, extent, cuts, smallest, top_value):
    loudness, own = 1.0, jax.random.fold_in(own_key, 6)
    for dim, shards_of in cuts:
        draws = jnp.exp(jax.random.uniform(jax.random.fold_in(own, dim), (shards_of,), jnp.float32, smallest / len(cuts), top_value / len(cuts)))
        loudness = loudness * jnp.repeat(draws, extent[dim] // shards_of).reshape([-1 if axis == dim else 1 for axis in range(len(extent))])
    return loudness


def bell_draw(stream_key, shape, spread, reach, cuts=(), held_as=jnp.bfloat16):
    result = jax.random.normal(stream_key, shape, jnp.float32) * spread
    if len(cuts) > 0:
        result = steps_of(stream_key, shape, cuts, -0.22, 0.18) * result
    return jnp.clip(result, min=-reach, max=reach).astype(held_as)


def setup_inputs(seed: int = 0) -> dict:
    key_of = jax.random.split(jax.random.key(seed), 9)
    tokens = bell_draw(key_of[0], (TOKENS, D), 1.0, 6.0, ((0, 128),))
    cotangent = bell_draw(key_of[1], (TOKENS, D), 1.0, 6.0, ((0, 128),))
    chosen = draw_chosen(jax.random.fold_in(key_of[8], 71), 0)
    counts = draw_counts(jax.random.fold_in(key_of[8], 71), 0)
    gate_prob = jnp.clip(0.049804688 + 0.9501953 * jax.random.uniform(key_of[4], (SOURCES, EXPERTS, M), jnp.float32) ** steps_of(key_of[4], (SOURCES, EXPERTS, M), ((0, 128),), -0.2, 0.2), 0.049804688, 1.0).astype(jnp.bfloat16)
    w_gate = bell_draw(key_of[5], (EXPERTS, D, FF), D ** -0.5, 0.09375, ((0, 8), (2, 16)))
    w_up = bell_draw(key_of[6], (EXPERTS, D, FF), D ** -0.5, 0.09375, ((0, 8), (2, 16)))
    w_down = bell_draw(key_of[7], (EXPERTS, FF, D), FF ** -0.5, 0.0625, ((0, 8), (1, 16)))
    return dict(tokens=tokens, cotangent=cotangent, chosen=chosen, counts=counts, gate_prob=gate_prob, w_gate=w_gate, w_up=w_up, w_down=w_down)


def expert_pass(inputs, scaled, w_gate, w_up, w_down):
    pre_gate = jnp.dot(inputs, w_gate, preferred_element_type=jnp.float32)
    pre_up = jnp.dot(inputs, w_up, preferred_element_type=jnp.float32)
    sigmoid = jax.nn.sigmoid(pre_gate)
    swish = pre_gate * sigmoid
    swish_slope = sigmoid * (1.0 + pre_gate * (1.0 - sigmoid))
    hidden = (swish * pre_up).astype(jnp.bfloat16)
    expert_out = jnp.dot(hidden, w_down, preferred_element_type=jnp.float32)
    hidden_grad = lax.dot_general(scaled, w_down, (((1,), (1,)), ((), ())), preferred_element_type=jnp.float32)
    pre_gate_grad = (hidden_grad * pre_up * swish_slope).astype(jnp.bfloat16)
    pre_up_grad = (hidden_grad * swish).astype(jnp.bfloat16)
    grad_gate = lax.dot_general(inputs, pre_gate_grad, (((0,), (0,)), ((), ())), preferred_element_type=jnp.float32)
    grad_up = lax.dot_general(inputs, pre_up_grad, (((0,), (0,)), ((), ())), preferred_element_type=jnp.float32)
    grad_down = lax.dot_general(hidden, scaled, (((0,), (0,)), ((), ())), preferred_element_type=jnp.float32)
    row_grad = lax.dot_general(pre_gate_grad, w_gate, (((1,), (1,)), ((), ())), preferred_element_type=jnp.float32)
    row_grad = row_grad + lax.dot_general(pre_up_grad, w_up, (((1,), (1,)), ((), ())), preferred_element_type=jnp.float32)
    return expert_out, row_grad, grad_gate.astype(jnp.bfloat16), grad_up.astype(jnp.bfloat16), grad_down.astype(jnp.bfloat16)


def reference(tokens, cotangent, chosen, counts, gate_prob, w_gate, w_up, w_down):
    sources = chosen.shape[0]
    tok_per = tokens.shape[0] // sources
    slot_iota = jnp.arange(chosen.shape[2], dtype=jnp.int32)
    is_live = slot_iota[None, None, :] < counts[:, :, None]
    gate_used = jnp.where(is_live, gate_prob.astype(jnp.float32), jnp.float32(0.0))
    global_index = (chosen + (jnp.arange(sources, dtype=jnp.int32) * tok_per)[:, None, None]).astype(jnp.int32)

    def one_expert(carry, packed):
        index_col, weight_col, live_col, gate_mat, up_mat, down_mat = packed
        flat_index = index_col.reshape(-1)
        row_weights = weight_col.reshape(-1)
        rows_in = tokens[flat_index]
        cot_rows = cotangent[flat_index].astype(jnp.float32)
        scaled = (row_weights[:, None] * cot_rows).astype(jnp.bfloat16)
        results = expert_pass(rows_in, scaled, gate_mat, up_mat, down_mat)
        comb_acc, grad_acc = carry
        comb_acc = comb_acc.at[flat_index].add(row_weights[:, None] * results[0])
        grad_acc = grad_acc.at[flat_index].add(results[1])
        probs = jnp.where(live_col.reshape(-1), jnp.sum(cot_rows * results[0], axis=-1), jnp.float32(0.0))
        return (comb_acc, grad_acc), (probs, results[2], results[3], results[4])

    start = (jnp.zeros(tokens.shape, jnp.float32), jnp.zeros(tokens.shape, jnp.float32))
    packed_all = (global_index.transpose(1, 0, 2), gate_used.transpose(1, 0, 2), is_live.transpose(1, 0, 2), w_gate, w_up, w_down)
    (comb_acc, grad_acc), stacked = lax.scan(one_expert, start, packed_all)
    probs, grad_gate, grad_up, grad_down = stacked
    prob_grad = probs.reshape(chosen.shape[1], sources, chosen.shape[2]).transpose(1, 0, 2)
    return comb_acc.astype(jnp.bfloat16), grad_acc.astype(jnp.bfloat16), prob_grad.astype(jnp.bfloat16), grad_gate, grad_up, grad_down
```

```python
import functools

import jax
import jax.numpy as jnp
from jax import lax
from jax.experimental import pallas as pl
from jax.experimental.pallas import tpu as pltpu
from jax.sharding import PartitionSpec as P

MESH = pl.DeviceIdType.MESH
BF = jnp.bfloat16
F32 = jnp.float32

D = 4096
HID = 448
TOK = 128
EXP = 8
PL = 16
SIDE = 4
M = 4
ROWS = 16
LIVE = ROWS * PL
Q = D // 4
H = D // 2


def dot(a, b, contract):
    return lax.dot_general(
        a, b, (((contract[0],), (contract[1],)), ((), ())), preferred_element_type=F32
    )


def iota(shape, dim):
    return lax.broadcasted_iota(jnp.int32, shape, dim)


def lanes256(tile):
    return jnp.concatenate([tile, tile], axis=1)[0:1, :]


def main_kernel(
    pidx_ref, pw_ref, cnt_ref, tok_hbm, cot_hbm, wg_hbm, wu_hbm, wd_hbm,
    t_out, s_out, hid_ref, pgg_ref, pug_ref, zr_ref,
    x_in, wg, wu, wd, csend, crecv, lsend, lrecv,
    zsend, zrecv, xsend, xrecv, esend, erecv, zsback, zrback,
    tbuf, sbuf, po, pr, r1, r2, r3, r4, qmat, fmat,
    in_sem, w_sem, out_sem, c_ss, c_rs, l_ss, l_rs, z_ss, z_rs, x_ss, x_rs,
    e_ss, e_rs, b_ss, b_rs, ag_ss, ag_rs, rs_ss, rs_rs,
):
    dp = lax.axis_index("dp")
    ex = lax.axis_index("expert")
    x, y = dp % SIDE, dp // SIDE

    def at_z(k):
        return (ex + k) % EXP

    def at_p(k):
        return (dp + k) % PL

    loads = []
    for a, src in enumerate((tok_hbm, cot_hbm)):
        for q in range(4):
            loads.append(
                pltpu.make_async_copy(
                    src.at[:, pl.ds(q * Q, Q)], x_in.at[a * 4 + q], in_sem.at[a * 4 + q]
                )
            )
    for c in loads:
        c.start()
    barrier = pltpu.get_barrier_semaphore()

    def greet_z(k, _):
        pl.semaphore_signal(barrier, inc=1, device_id=(dp, at_z(k)), device_id_type=MESH)
        return 0

    def greet_p(k, _):
        pl.semaphore_signal(barrier, inc=1, device_id=(at_p(k), ex), device_id_type=MESH)
        return 0

    lax.fori_loop(1, EXP, greet_z, 0)
    lax.fori_loop(1, PL, greet_p, 0)
    wcopies = [
        pltpu.make_async_copy(src, dst, w_sem.at[i])
        for i, (src, dst) in enumerate(((wg_hbm, wg), (wu_hbm, wu), (wd_hbm, wd)))
    ]

    csend[...] = cnt_ref[...]
    pick = jnp.where(
        iota((256, 8 * TOK), 1) == pidx_ref[...], pw_ref[...], F32(0.0)
    ).astype(BF)
    for c in loads:
        c.wait()
    for c in wcopies:
        c.start()
    zsend[...] = (
        dot(pick, x_in[...].reshape(8 * TOK, Q), (1, 0)).astype(BF).reshape(EXP, 32, Q)
    )
    pl.semaphore_wait(barrier, EXP - 1 + PL - 1)

    def c_copy(k, src, dst, peer):
        return pltpu.make_async_remote_copy(
            src_ref=csend.at[src], dst_ref=crecv.at[dst], send_sem=c_ss.at[k],
            recv_sem=c_rs.at[k], device_id=(dp, peer), device_id_type=MESH,
        )

    def z_copy(k, src, dst, peer):
        return pltpu.make_async_remote_copy(
            src_ref=zsend.at[src], dst_ref=zrecv.at[dst], send_sem=z_ss.at[k],
            recv_sem=z_rs.at[k], device_id=(dp, peer), device_id_type=MESH,
        )

    def start_c(k, _):
        c_copy(k, at_z(k), ex, at_z(k)).start()
        return 0

    def start_z(k, _):
        z_copy(k, at_z(k), ex, at_z(k)).start()
        return 0

    lax.fori_loop(1, EXP, start_c, 0)
    lax.fori_loop(1, EXP, start_z, 0)
    crecv[ex] = csend[ex]
    zrecv[ex] = zsend[ex]

    def wait_c(k, _):
        c_copy(k, at_z(k), at_z(EXP - k), at_z(k)).wait_recv()
        return 0

    lax.fori_loop(1, EXP, wait_c, 0)

    total = crecv[0]
    for s in range(1, EXP):
        total = total + crecv[s]
    lsend[...] = total
    lrecv[dp] = total

    def l_copy(k, dst, peer):
        return pltpu.make_async_remote_copy(
            src_ref=lsend, dst_ref=lrecv.at[dst], send_sem=l_ss.at[k],
            recv_sem=l_rs.at[k], device_id=(peer, ex), device_id_type=MESH,
        )

    def start_l(k, _):
        l_copy(k, dp, at_p(k)).start()
        return 0

    def wait_l(k, _):
        l_copy(k, at_p(PL - k), at_p(k)).wait_recv()
        return 0

    lax.fori_loop(1, PL, start_l, 0)

    lane = iota((8, 256), 1)
    src = lane // 32
    prefix = jnp.zeros((8, 256), jnp.int32)
    own = jnp.zeros((8, 256), jnp.int32)
    for s in range(EXP):
        v = jnp.concatenate([crecv[s], crecv[s]], axis=1)
        prefix = prefix + jnp.where(src > s, v, 0)
        own = jnp.where(src == s, v, own)
    slot = lane % M
    rank = jnp.where(slot < own, prefix + slot, -1)[0:1, :]

    lax.fori_loop(1, PL, wait_l, 0)
    zero = jnp.zeros((8, 128), jnp.int32)
    before = zero
    col = lane // ROWS
    off_l = jnp.zeros((8, 256), jnp.int32)
    len_l = jnp.zeros((8, 256), jnp.int32)
    running = zero
    for i in range(PL):
        v = lrecv[i]
        off_l = jnp.where(col == i, jnp.concatenate([running, running], axis=1), off_l)
        len_l = jnp.where(col == i, jnp.concatenate([v, v], axis=1), len_l)
        before = before + jnp.where(i < dp, v, zero)
        running = running + v
    offset = lanes256(before)
    r_l = ((dp - off_l + 512) & (ROWS - 1)) + ROWS * (lane % 2)
    pos = jnp.where(r_l < len_l, (off_l + r_l) // ROWS, -1)[0:1, :]

    row = iota((256, 256), 0)
    clane = iota((256, 256), 1)
    want = ((row // ROWS - offset + 512) & (ROWS - 1)) + ROWS * (row % 2)
    same = ((row // 4) % 4 == (clane // 8) % 4) & ((row // 2) % 2 == (clane // 4) % 2)
    qmat[...] = jnp.where(same & (want == rank), F32(1.0), F32(0.0)).astype(BF)
    frow = iota((128, 256), 0)
    flane = iota((128, 256), 1)
    fsame = (frow // 64 == (flane // 2) % 2) & ((frow // 16) % 4 == (flane // 4) % 4)
    fmat[...] = jnp.where(fsame & (frow % 16 == pos), F32(1.0), F32(0.0)).astype(BF)

    def wait_z(k, _):
        z_copy(k, at_z(k), at_z(EXP - k), at_z(k)).wait_recv()
        return 0

    lax.fori_loop(1, EXP, wait_z, 0)
    xsend[...] = (
        dot(qmat[...], zrecv[...].reshape(256, Q), (1, 0)).astype(BF).reshape(PL, ROWS, Q)
    )

    def x_copy(k, src, dst, peer):
        return pltpu.make_async_remote_copy(
            src_ref=xsend.at[src], dst_ref=xrecv.at[dst], send_sem=x_ss.at[k],
            recv_sem=x_rs.at[k], device_id=(peer, ex), device_id_type=MESH,
        )

    def start_x(k, _):
        x_copy(k, at_p(k), dp, at_p(k)).start()
        return 0

    def wait_x(k, _):
        x_copy(k, at_p(k), at_p(PL - k), at_p(k)).wait_recv()
        return 0

    lax.fori_loop(1, PL, start_x, 0)
    xrecv[dp] = xsend[dp]
    lax.fori_loop(1, PL, wait_x, 0)
    mine = dot(fmat[...], xrecv[...].reshape(256, Q), (1, 0)).astype(BF)
    for q in range(4):
        tbuf[dp, :, pl.ds(q * Q, Q)] = mine[q * 16 : q * 16 + 16]
        sbuf[dp, :, pl.ds(q * Q, Q)] = mine[64 + q * 16 : 64 + q * 16 + 16]

    def up(v, o):
        return (v + o + SIDE) % SIDE

    def index(part, u, v):
        return v * SIDE + u if part == 0 else u * SIDE + v

    def device(part, du, dv):
        if part == 0:
            return (up(y, dv) * SIDE + up(x, du), ex)
        return (up(y, du) * SIDE + up(x, dv), ex)

    gathered = (tbuf, sbuf)
    uv = ((x, y), (y, x))
    sent = []

    def ag(part, ident, block, half, du, dv):
        ref = gathered[part].at[block]
        if half is not None:
            ref = ref.at[:, pl.ds(half * H, H)]
        return pltpu.make_async_remote_copy(
            src_ref=ref, dst_ref=ref, send_sem=ag_ss.at[part, ident],
            recv_sem=ag_rs.at[part, ident], device_id=device(part, du, dv), device_id_type=MESH,
        )

    def ag_send(*args):
        c = ag(*args)
        c.start()
        sent.append(c)

    sign = (1, -1)

    def block_of(part, o, ov):
        u, v = uv[part]
        return index(part, up(u, o), up(v, ov))

    def phase2(part, o):
        for d in range(2):
            ag_send(part, 4 + o * 4 + d, block_of(part, o, 0), None, 0, sign[d])

    def pass_on2(part, o):
        for d in range(2):
            b = block_of(part, o, -sign[d])
            ag(part, 4 + o * 4 + d, b, None, 0, sign[d]).wait_recv()
            ag_send(part, 4 + o * 4 + 2 + d, b, d, 0, sign[d])

    for part in range(2):
        for d in range(2):
            ag_send(part, d, block_of(part, 0, 0), None, sign[d], 0)
        phase2(part, 0)
    for part in range(2):
        for d in range(2):
            o = 3 if d == 0 else 1
            b = block_of(part, o, 0)
            ag(part, d, b, None, sign[d], 0).wait_recv()
            ag_send(part, 2 + d, b, d, sign[d], 0)
            phase2(part, o)
    for part in range(2):
        pass_on2(part, 0)
    for part in range(2):
        for d in range(2):
            ag(part, 2 + d, block_of(part, 2, 0), d, sign[d], 0).wait_recv()
        phase2(part, 2)
    for o in (3, 1, 2):
        for part in range(2):
            pass_on2(part, o)
    for o in (0, 3, 1, 2):
        for part in range(2):
            for d in range(2):
                ag(part, 4 + o * 4 + 2 + d, block_of(part, o, 2), d, 0, sign[d]).wait_recv()

    outs = [
        pltpu.make_async_copy(tbuf, t_out, out_sem.at[0]),
        pltpu.make_async_copy(sbuf, s_out, out_sem.at[1]),
    ]
    for c in outs:
        c.start()

    for c in wcopies:
        c.wait()
    rows_in = tbuf[...].reshape(LIVE, D)
    pre_gate = dot(rows_in, wg[...], (1, 0))
    pre_up = dot(rows_in, wu[...], (1, 0))
    hidden_grad = dot(sbuf[...].reshape(LIVE, D), wd[...], (1, 1))
    sig = jax.nn.sigmoid(pre_gate)
    swish = pre_gate * sig
    slope = sig * (1.0 + pre_gate * (1.0 - sig))
    hid_ref[...] = (swish * pre_up).astype(BF)
    pgg_ref[...] = (hidden_grad * pre_up * slope).astype(BF)
    pug_ref[...] = (hidden_grad * swish).astype(BF)

    partial = (po, pr)
    WIDE = 512

    def second(n, _):
        cols = pl.ds(pl.multiple_of(n * WIDE, WIDE), WIDE)
        po[:, :, :, cols] = (
            dot(hid_ref[...], wd[:, cols], (1, 0)).astype(BF).reshape(SIDE, SIDE, ROWS, WIDE)
        )
        grad = dot(pgg_ref[...], wg[cols, :], (1, 1)) + dot(pug_ref[...], wu[cols, :], (1, 1))
        pr[:, :, :, cols] = grad.astype(BF).reshape(SIDE, SIDE, ROWS, WIDE)
        return 0

    def cols_of(half):
        return pl.ds(half * H, H)

    def group(part, ov):
        v = up(uv[part][1], ov)
        return partial[part].at[v] if part == 0 else partial[part].at[:, v]

    def piece(part, ou):
        u, v = up(uv[part][0], ou), uv[part][1]
        return partial[part].at[v, u] if part == 0 else partial[part].at[u, v]

    def rs(part, ident, src, dst, du, dv):
        return pltpu.make_async_remote_copy(
            src_ref=src, dst_ref=dst, send_sem=rs_ss.at[part, ident],
            recv_sem=rs_rs.at[part, ident], device_id=device(part, du, dv), device_id_type=MESH,
        )

    def far(part, d):
        return rs(part, d, group(part, 2).at[:, :, cols_of(d)], r1.at[part, d], 0, sign[d])

    def near(part, d, h):
        return rs(
            part, 2 + 2 * d + h, group(part, sign[d]).at[:, :, cols_of(h)],
            r2.at[part, d, h], 0, sign[d],
        )

    def far1(part, d):
        return rs(part, 6 + d, piece(part, 2).at[:, cols_of(d)], r3.at[part, d], sign[d], 0)

    def near1(part, d, h):
        return rs(
            part, 8 + 2 * d + h, piece(part, sign[d]).at[:, cols_of(h)],
            r4.at[part, d, h], sign[d], 0,
        )

    def go(c):
        c.start()
        sent.append(c)

    for h in range(2):
        lax.fori_loop(h * 4, h * 4 + 4, second, 0)
        for part in range(2):
            go(far(part, h))
        for part in range(2):
            go(near(part, 1 - h, h))
    for d in range(2):
        for part in range(2):
            far(part, d).wait_recv()
            ref = group(part, sign[d]).at[:, :, cols_of(d)]
            ref[...] = (ref[...].astype(F32) + r1[part, d].astype(F32)).astype(BF)
            go(near(part, d, d))
    for part in range(2):
        for d in range(2):
            for h in range(2):
                near(part, d, h).wait_recv()
        for o in (2, 1, 3, 0):
            u = up(uv[part][0], o)
            for h in range(2):
                ref = piece(part, o).at[:, cols_of(h)]
                ref[...] = (
                    ref[...].astype(F32)
                    + r2[part, 0, h, u].astype(F32)
                    + r2[part, 1, h, u].astype(F32)
                ).astype(BF)
            if o == 2:
                go(far1(part, 0))
                go(far1(part, 1))
            elif o != 0:
                d = 0 if o == 1 else 1
                go(near1(part, d, 1 - d))
    for part in range(2):
        for d in range(2):
            far1(part, d).wait_recv()
            ref = piece(part, sign[d]).at[:, cols_of(d)]
            ref[...] = (ref[...].astype(F32) + r3[part, d].astype(F32)).astype(BF)
            go(near1(part, d, d))
    reduced = []
    for part in range(2):
        for h in range(2):
            for d in range(2):
                near1(part, d, h).wait_recv()
            full = (
                piece(part, 0)[:, cols_of(h)].astype(F32)
                + r4[part, 0, h].astype(F32)
                + r4[part, 1, h].astype(F32)
            ).astype(BF)
            reduced += [full[:, :Q], full[:, Q:]]

    esend[...] = (
        dot(fmat[...], jnp.concatenate(reduced, axis=0), (0, 0)).astype(BF).reshape(PL, ROWS, Q)
    )

    def e_copy(k, src, dst, peer):
        return pltpu.make_async_remote_copy(
            src_ref=esend.at[src], dst_ref=erecv.at[dst], send_sem=e_ss.at[k],
            recv_sem=e_rs.at[k], device_id=(peer, ex), device_id_type=MESH,
        )

    def start_e(k, _):
        e_copy(k, at_p(k), dp, at_p(k)).start()
        return 0

    def wait_e(k, _):
        e_copy(k, at_p(k), at_p(PL - k), at_p(k)).wait_recv()
        return 0

    lax.fori_loop(1, PL, start_e, 0)
    erecv[dp] = esend[dp]
    lax.fori_loop(1, PL, wait_e, 0)
    zsback[...] = (
        dot(qmat[...], erecv[...].reshape(256, Q), (0, 0)).astype(BF).reshape(EXP, 32, Q)
    )

    def b_copy(k, src, dst, peer):
        return pltpu.make_async_remote_copy(
            src_ref=zsback.at[src], dst_ref=zrback.at[dst], send_sem=b_ss.at[k],
            recv_sem=b_rs.at[k], device_id=(dp, peer), device_id_type=MESH,
        )

    def start_b(k, _):
        b_copy(k, at_z(k), ex, at_z(k)).start()
        return 0

    def wait_b(k, _):
        b_copy(k, at_z(k), at_z(EXP - k), at_z(k)).wait_recv()
        return 0

    lax.fori_loop(1, EXP, start_b, 0)
    zrback[ex] = zsback[ex]
    lax.fori_loop(1, EXP, wait_b, 0)
    zr_ref[...] = zrback[...].reshape(256, Q)

    def done_z(k, _):
        c_copy(k, at_z(k), ex, at_z(k)).wait_send()
        z_copy(k, at_z(k), ex, at_z(k)).wait_send()
        b_copy(k, at_z(k), ex, at_z(k)).wait_send()
        return 0

    def done_p(k, _):
        l_copy(k, dp, at_p(k)).wait_send()
        x_copy(k, at_p(k), dp, at_p(k)).wait_send()
        e_copy(k, at_p(k), dp, at_p(k)).wait_send()
        return 0

    lax.fori_loop(1, EXP, done_z, 0)
    lax.fori_loop(1, PL, done_p, 0)
    for c in sent:
        c.wait_send()
    for c in outs:
        c.wait()


def run_main(pidx, pw, cnt, tokens, cotangent, wg, wu, wd):
    vmem = pl.BlockSpec(memory_space=pltpu.VMEM)
    anym = pl.BlockSpec(memory_space=pl.ANY)
    dma = pltpu.SemaphoreType.DMA
    return pl.pallas_call(
        main_kernel,
        out_shape=(
            jax.ShapeDtypeStruct((PL, ROWS, D), BF),
            jax.ShapeDtypeStruct((PL, ROWS, D), BF),
            jax.ShapeDtypeStruct((LIVE, HID), BF),
            jax.ShapeDtypeStruct((LIVE, HID), BF),
            jax.ShapeDtypeStruct((LIVE, HID), BF),
            jax.ShapeDtypeStruct((256, Q), BF),
        ),
        in_specs=[vmem] * 3 + [anym] * 5,
        out_specs=(anym, anym, vmem, vmem, vmem, vmem),
        scratch_shapes=[
            pltpu.VMEM((8, TOK, Q), BF),
            pltpu.VMEM((D, HID), BF),
            pltpu.VMEM((D, HID), BF),
            pltpu.VMEM((HID, D), BF),
            pltpu.VMEM((EXP, 8, 128), jnp.int32),
            pltpu.VMEM((EXP, 8, 128), jnp.int32),
            pltpu.VMEM((8, 128), jnp.int32),
            pltpu.VMEM((PL, 8, 128), jnp.int32),
            pltpu.VMEM((EXP, 32, Q), BF),
            pltpu.VMEM((EXP, 32, Q), BF),
            pltpu.VMEM((PL, ROWS, Q), BF),
            pltpu.VMEM((PL, ROWS, Q), BF),
            pltpu.VMEM((PL, ROWS, Q), BF),
            pltpu.VMEM((PL, ROWS, Q), BF),
            pltpu.VMEM((EXP, 32, Q), BF),
            pltpu.VMEM((EXP, 32, Q), BF),
            pltpu.VMEM((PL, ROWS, D), BF),
            pltpu.VMEM((PL, ROWS, D), BF),
            pltpu.VMEM((SIDE, SIDE, ROWS, D), BF),
            pltpu.VMEM((SIDE, SIDE, ROWS, D), BF),
            pltpu.VMEM((2, 2, SIDE, ROWS, H), BF),
            pltpu.VMEM((2, 2, 2, SIDE, ROWS, H), BF),
            pltpu.VMEM((2, 2, ROWS, H), BF),
            pltpu.VMEM((2, 2, 2, ROWS, H), BF),
            pltpu.VMEM((256, 256), BF),
            pltpu.VMEM((128, 256), BF),
            dma((8,)),
            dma((3,)),
            dma((2,)),
            dma((EXP,)),
            dma((EXP,)),
            dma((PL,)),
            dma((PL,)),
            dma((EXP,)),
            dma((EXP,)),
            dma((PL,)),
            dma((PL,)),
            dma((PL,)),
            dma((PL,)),
            dma((EXP,)),
            dma((EXP,)),
            dma((2, 20)),
            dma((2, 20)),
            dma((2, 12)),
            dma((2, 12)),
        ],
        compiler_params=pltpu.CompilerParams(
            collective_id=0, has_side_effects=True, vmem_limit_bytes=58 * 1024 * 1024
        ),
        cost_estimate=pl.CostEstimate(
            flops=6 * 2 * LIVE * D * HID, bytes_accessed=20 << 20, transcendentals=LIVE * HID
        ),
        name="routed_experts",
    )(pidx, pw, cnt, tokens, cotangent, wg, wu, wd)


TILE = 512


def tail_kernel(
    cidx_ref, cw_ref, clive_ref, t_ref, s_ref, hid_ref, pgg_ref, pug_ref, zr_ref, cot_ref,
    comb_ref, tg_ref, prob_ref, gg_ref, gu_ref, gd_ref,
):
    step = pl.program_id(0)
    tile = t_ref[...]
    gg_ref[...] = dot(tile, pgg_ref[...], (0, 0)).astype(BF)
    gu_ref[...] = dot(tile, pug_ref[...], (0, 0)).astype(BF)
    gd_ref[...] = dot(hid_ref[...], s_ref[...], (0, 0)).astype(BF)

    q = step // (Q // TILE)
    r = iota((64, 256), 0)
    c = iota((64, 256), 1)
    target = (((r % 32) // 4) * 4 + q) * 8 + (r // 32) * 4 + r % 4
    rows = dot(jnp.where(c == target, F32(1.0), F32(0.0)).astype(BF), zr_ref[...], (1, 0))
    out_rows = rows[:32]
    grad_rows = rows[32:]
    match = iota((32, TOK), 1) == cidx_ref[...]
    pick_w = jnp.where(match, cw_ref[...], F32(0.0)).astype(BF)
    pick_live = jnp.where(match, clive_ref[...], F32(0.0)).astype(BF)
    comb_ref[...] = dot(pick_w, out_rows.astype(BF), (0, 0)).astype(BF)
    tg_ref[...] = dot(pick_live, grad_rows.astype(BF), (0, 0)).astype(BF)
    cot_rows = dot(pick_live, cot_ref[...], (1, 0))
    prod = cot_rows * out_rows
    part = prod[:, 0:128]
    for i in range(1, TILE // 128):
        part = part + prod[:, i * 128 : (i + 1) * 128]

    @pl.when(step == 0)
    def _():
        prob_ref[...] = jnp.zeros_like(prob_ref)

    prob_ref[...] += part


def run_tail(cidx, cw, clive, t, s, hid, pgg, pug, zr, cotangent):
    def whole(shape):
        return pl.BlockSpec(shape, lambda i: (0, 0))

    per_q = Q // TILE
    return pl.pallas_call(
        tail_kernel,
        grid=(D // TILE,),
        out_shape=(
            jax.ShapeDtypeStruct((TOK, D), BF),
            jax.ShapeDtypeStruct((TOK, D), BF),
            jax.ShapeDtypeStruct((32, 128), F32),
            jax.ShapeDtypeStruct((D, HID), BF),
            jax.ShapeDtypeStruct((D, HID), BF),
            jax.ShapeDtypeStruct((HID, D), BF),
        ),
        in_specs=[
            whole((32, 1)),
            whole((32, 1)),
            whole((32, 1)),
            pl.BlockSpec((LIVE, TILE), lambda i: (0, i)),
            pl.BlockSpec((LIVE, TILE), lambda i: (0, i)),
            whole((LIVE, HID)),
            whole((LIVE, HID)),
            whole((LIVE, HID)),
            pl.BlockSpec((256, TILE), lambda i: (0, i % per_q)),
            pl.BlockSpec((TOK, TILE), lambda i: (0, i)),
        ],
        out_specs=(
            pl.BlockSpec((TOK, TILE), lambda i: (0, i)),
            pl.BlockSpec((TOK, TILE), lambda i: (0, i)),
            whole((32, 128)),
            pl.BlockSpec((TILE, HID), lambda i: (i, 0)),
            pl.BlockSpec((TILE, HID), lambda i: (i, 0)),
            pl.BlockSpec((HID, TILE), lambda i: (0, i)),
        ),
        compiler_params=pltpu.CompilerParams(vmem_limit_bytes=40 * 1024 * 1024),
        cost_estimate=pl.CostEstimate(
            flops=3 * 2 * LIVE * D * HID, bytes_accessed=20 << 20, transcendentals=0
        ),
        name="weight_grads_and_combine",
    )(cidx, cw, clive, t, s, hid, pgg, pug, zr, cotangent)


def per_device(tokens, cotangent, chosen, counts, gate_prob, w_gate, w_up, w_down):
    chosen_here = chosen[0]
    slot_iota = lax.broadcasted_iota(jnp.int32, (EXP, M), 1)
    is_live = slot_iota < counts[0][:, None]
    weights = jnp.where(is_live, gate_prob[0].astype(F32), F32(0.0))
    piece = lax.broadcasted_iota(jnp.int32, (EXP, 4, 2, M), 1)
    array = lax.broadcasted_iota(jnp.int32, (EXP, 4, 2, M), 2)
    pidx = ((array * 4 + piece) * TOK + chosen_here[:, None, None, :]).reshape(256, 1)
    pw = jnp.where(array == 0, F32(1.0), weights[:, None, None, :]).reshape(256, 1)
    cnt = jnp.broadcast_to(counts[0][:, None, None], (EXP, 8, 128))
    t, s, hid, pgg, pug, zr = run_main(
        pidx, pw, cnt, tokens, cotangent, w_gate[0], w_up[0], w_down[0]
    )
    combined, token_grad, prob, gg, gu, gd = run_tail(
        chosen_here.reshape(32, 1),
        weights.reshape(32, 1),
        is_live.astype(F32).reshape(32, 1),
        t.reshape(LIVE, D),
        s.reshape(LIVE, D),
        hid,
        pgg,
        pug,
        zr,
        cotangent,
    )
    inner = jnp.sum(prob, axis=-1).reshape(EXP, M)
    prob_grad = jnp.where(is_live, inner, F32(0.0)).astype(BF)
    return combined, token_grad, prob_grad[None], gg[None], gu[None], gd[None]


def solution(mesh):
    tokens = P(("dp", "expert"), None)
    slots = P(("dp", "expert"), None, None)
    specs = (tokens, tokens, slots, tokens, slots)
    weights = (P("expert", None, "dp"), P("expert", None, "dp"), P("expert", "dp", None))
    return jax.shard_map(
        per_device,
        mesh=mesh,
        in_specs=specs + weights,
        out_specs=(tokens, tokens, slots) + weights,
        check_vma=False,
    )
```

```python
import functools

import jax
import jax.numpy as jnp
from jax import lax
from jax.experimental import pallas as pl
from jax.experimental.pallas import tpu as pltpu
from jax.sharding import PartitionSpec as P

MESH = pl.DeviceIdType.MESH
BF = jnp.bfloat16
F32 = jnp.float32

D = 4096
HID = 448
TOK = 128
EXP = 8
PL = 16
SIDE = 4
M = 4
ROWS = 16
LIVE = ROWS * PL
HALVES = 2
W = D // HALVES
Q = W // 4
H = W // 2


def dot(a, b, contract):
    return lax.dot_general(
        a, b, (((contract[0],), (contract[1],)), ((), ())), preferred_element_type=F32
    )


def iota(shape, dim):
    return lax.broadcasted_iota(jnp.int32, shape, dim)


def of_rows(expert, m, chosen_ref, gate_ref, cnt_ref):
    chosen = jnp.zeros(m.shape, F32)
    gate = jnp.zeros(m.shape, F32)
    for i in range(M):
        chosen = jnp.where(m == i, chosen_ref[i : i + 1, :].astype(F32), chosen)
        gate = jnp.where(m == i, gate_ref[i : i + 1, :].astype(F32), gate)
    here = iota(m.shape, 1) == expert
    live = here & (m < cnt_ref[...])

    def take(v, mask):
        return jnp.sum(jnp.where(mask, v, F32(0.0)), axis=1, keepdims=True)

    return take(chosen, here).astype(jnp.int32), take(gate, live), take(F32(1.0), live)


def main_kernel(
    chosen_ref, gate_ref, cnt_ref, cnt_smem, tok_hbm, cot_hbm, wg_hbm, wu_hbm, wd_hbm,
    t_out, s_out, hid_t, pgg_t, pug_t, zr_ref,
    x_in, wg, wu, wd, csend, crecv, lsend, lrecv,
    zsend, zrecv, xsend, xrecv, esend, erecv, zsback, zrback,
    tbuf, sbuf, gate_acc, up_acc, grad_acc, hid, pgg, pug, turned, po, pr, r1, r2, r3, r4, qmat, fmat,
    in_sem, w_sem, out_sem, act_sem, c_ss, c_rs, l_ss, l_rs, z_ss, z_rs, x_ss, x_rs,
    e_ss, e_rs, b_ss, b_rs, ag_ss, ag_rs, rs_ss, rs_rs,
):
    dp = lax.axis_index("dp")
    ex = lax.axis_index("expert")
    x, y = lax.rem(dp, SIDE), lax.div(dp, SIDE)
    halves = range(HALVES)

    def at_z(k):
        return lax.rem(ex + k, EXP)

    def at_p(k):
        return lax.rem(dp + k, PL)

    def each(count, body):
        def step(k, _):
            body(k)
            return 0

        lax.fori_loop(1, count, step, 0)

    loads = [
        [
            pltpu.make_async_copy(
                src.at[:, pl.ds(h * W + q * Q, Q)], x_in.at[h, a * 4 + q], in_sem.at[h, a * 4 + q]
            )
            for a, src in enumerate((tok_hbm, cot_hbm))
            for q in range(4)
        ]
        for h in halves
    ]
    for h in halves:
        for c in loads[h]:
            c.start()
    barrier = pltpu.get_barrier_semaphore()

    def greet(device):
        pl.semaphore_signal(barrier, inc=1, device_id=device, device_id_type=MESH)

    each(EXP, lambda k: greet((dp, at_z(k))))
    each(PL, lambda k: greet((at_p(k), ex)))
    wcopies = [
        pltpu.make_async_copy(src, dst, w_sem.at[i])
        for i, (src, dst) in enumerate(((wg_hbm, wg), (wu_hbm, wu), (wd_hbm, wd)))
    ]

    for e in range(EXP):
        csend[e] = jnp.full((8, 128), cnt_smem[0, e], jnp.int32)
    r = iota((256, EXP), 0)
    token, weight, _ = of_rows(r >> 5, r & 3, chosen_ref, gate_ref, cnt_ref)
    r = iota((256, 1), 0)
    token = token + (((r >> 2) & 1) * 4 + ((r >> 3) & 3)) * TOK
    weight = jnp.where((r & 4) == 0, F32(1.0), weight)
    pick = jnp.where(iota((256, 8 * TOK), 1) == token, weight, F32(0.0)).astype(BF)

    def remote(src, dst, ss, rs, device):
        return pltpu.make_async_remote_copy(
            src_ref=src, dst_ref=dst, send_sem=ss, recv_sem=rs, device_id=device,
            device_id_type=MESH,
        )

    def c_copy(k, dst):
        return remote(csend.at[at_z(k)], crecv.at[dst], c_ss.at[k], c_rs.at[k], (dp, at_z(k)))

    def z_copy(h, k, dst):
        return remote(
            zsend.at[h, at_z(k)], zrecv.at[h, dst], z_ss.at[h, k], z_rs.at[h, k], (dp, at_z(k))
        )

    def b_copy(h, k, dst):
        return remote(
            zsback.at[h, at_z(k)], zrback.at[h, dst], b_ss.at[h, k], b_rs.at[h, k], (dp, at_z(k))
        )

    def l_copy(k, dst):
        return remote(lsend, lrecv.at[dst], l_ss.at[k], l_rs.at[k], (at_p(k), ex))

    def x_copy(h, k, dst):
        return remote(
            xsend.at[h, at_p(k)], xrecv.at[h, dst], x_ss.at[h, k], x_rs.at[h, k], (at_p(k), ex)
        )

    def e_copy(h, k, dst):
        return remote(
            esend.at[h, at_p(k)], erecv.at[h, dst], e_ss.at[h, k], e_rs.at[h, k], (at_p(k), ex)
        )

    for h in halves:
        for c in loads[h]:
            c.wait()
        if h == HALVES - 1:
            for c in wcopies:
                c.start()
        zsend[h] = dot(pick, x_in[h].reshape(8 * TOK, Q), (1, 0)).astype(BF).reshape(EXP, 32, Q)
        if h == 0:
            pl.semaphore_wait(barrier, EXP - 1 + PL - 1)
            each(EXP, lambda k: c_copy(k, ex).start())
        each(EXP, lambda k, h=h: z_copy(h, k, ex).start())
        zrecv[h, ex] = zsend[h, ex]
    crecv[ex] = csend[ex]
    each(EXP, lambda k: c_copy(k, at_z(EXP - k)).wait_recv())

    total = crecv[0]
    for s in range(1, EXP):
        total = total + crecv[s]
    lsend[...] = total
    lrecv[dp] = total
    each(PL, lambda k: l_copy(k, dp).start())

    lane = iota((8, 256), 1)
    src = lane >> 5
    rank = lane & 3
    used = jnp.zeros((8, 256), jnp.int32)
    for s in range(EXP):
        v = jnp.concatenate([crecv[s], crecv[s]], axis=1)
        used = jnp.where(src == s, v, used)
        if s < EXP - 1:
            rank = rank + jnp.where(src > s, v, 0)
    alive = (lane & 3) < used

    each(PL, lambda k: l_copy(k, at_p(PL - k)).wait_recv())
    zero = jnp.zeros((8, 128), jnp.int32)
    before = zero
    col = lane >> 4
    off_l = jnp.zeros((8, 256), jnp.int32)
    len_l = jnp.zeros((8, 256), jnp.int32)
    running = zero
    for i in range(PL):
        v = lrecv[i]
        off_l = jnp.where(col == i, jnp.concatenate([running, running], axis=1), off_l)
        len_l = jnp.where(col == i, jnp.concatenate([v, v], axis=1), len_l)
        before = before + jnp.where(i < dp, v, zero)
        running = running + v
    dealt = rank + jnp.concatenate([before, before], axis=1)
    to = ((dealt & 15) << 4) + (((lane >> 3) & 3) << 2) + (((lane >> 2) & 1) << 1) + (rank >> 4)
    to = jnp.where(alive, to, -1)[0:1, :]
    qmat[...] = jnp.where(iota((256, 256), 0) == to, F32(1.0), F32(0.0)).astype(BF)
    own = ((dp - off_l + 512) & 15) + ((lane & 1) << 4)
    to = (((lane >> 1) & 1) << 6) + (((lane >> 2) & 3) << 4) + ((off_l + own) >> 4)
    to = jnp.where(own < len_l, to, -1)[0:1, :]
    fmat[...] = jnp.where(iota((128, 256), 0) == to, F32(1.0), F32(0.0)).astype(BF)

    for h in halves:
        each(EXP, lambda k, h=h: z_copy(h, k, at_z(EXP - k)).wait_recv())
        xsend[h] = (
            dot(qmat[...], zrecv[h].reshape(256, Q), (1, 0)).astype(BF).reshape(PL, ROWS, Q)
        )
        each(PL, lambda k, h=h: x_copy(h, k, dp).start())
        xrecv[h, dp] = xsend[h, dp]

    def compact(h):
        each(PL, lambda k: x_copy(h, k, at_p(PL - k)).wait_recv())
        mine = dot(fmat[...], xrecv[h].reshape(256, Q), (1, 0)).astype(BF)
        for q in range(4):
            tbuf[h, dp, :, pl.ds(q * Q, Q)] = mine[q * 16 : q * 16 + 16]
            sbuf[h, dp, :, pl.ds(q * Q, Q)] = mine[64 + q * 16 : 64 + q * 16 + 16]

    ups = [[lax.rem(v + o, SIDE) if o else v for o in range(SIDE)] for v in (x, y)]
    blocks = [[ups[1][oy] * SIDE + ups[0][ox] for ox in range(SIDE)] for oy in range(SIDE)]

    def block_of(part, ou, ov):
        ou, ov = ou % SIDE, ov % SIDE
        return blocks[ov][ou] if part == 0 else blocks[ou][ov]

    def device(part, du, dv):
        return (block_of(part, du, dv), ex)

    gathered = (tbuf, sbuf)
    sign = (1, -1)
    both = [(part, d) for part in range(2) for d in range(2)]
    sent = []

    def go(c):
        c.start()
        sent.append(c)

    def ag_steps(h):
        def ag(part, ident, block, half, du, dv):
            ref = gathered[part].at[h, block]
            if half is not None:
                ref = ref.at[:, pl.ds(half * H, H)]
            return remote(
                ref, ref, ag_ss.at[h, part, ident], ag_rs.at[h, part, ident], device(part, du, dv)
            )

        def phase2(part, o):
            for d in range(2):
                go(ag(part, 4 + o * 4 + d, block_of(part, o, 0), None, 0, sign[d]))

        def begin():
            for part in range(2):
                for d in range(2):
                    go(ag(part, d, block_of(part, 0, 0), None, sign[d], 0))
                phase2(part, 0)

        def near():
            for part, d in both:
                o = 3 if d == 0 else 1
                b = block_of(part, o, 0)
                ag(part, d, b, None, sign[d], 0).wait_recv()
                go(ag(part, 2 + d, b, d, sign[d], 0))
                phase2(part, o)

        def far():
            for part, d in both:
                ag(part, 2 + d, block_of(part, 2, 0), d, sign[d], 0).wait_recv()
            for part in range(2):
                phase2(part, 2)

        def pass_on(o):
            for part, d in both:
                b = block_of(part, o, -sign[d])
                ag(part, 4 + o * 4 + d, b, None, 0, sign[d]).wait_recv()
                go(ag(part, 4 + o * 4 + 2 + d, b, d, 0, sign[d]))

        def finish():
            for o in (0, 3, 1, 2):
                for part, d in both:
                    b = block_of(part, o, 2)
                    ag(part, 4 + o * 4 + 2 + d, b, d, 0, sign[d]).wait_recv()

        return begin, near, far, pass_on, finish

    outs = [
        [
            pltpu.make_async_copy(buf.at[h], out.at[h], out_sem.at[h, i])
            for i, (buf, out) in enumerate(((tbuf, t_out), (sbuf, s_out)))
        ]
        for h in halves
    ]

    def first(buf, w, h):
        return dot(buf[h].reshape(LIVE, W), w[:, pl.ds(h * W, W)], (1, 1))

    begin0, near0, far0, pass0, finish0 = ag_steps(0)
    begin1, near1, far1, pass1, finish1 = ag_steps(1)
    compact(0)
    begin0()
    compact(1)
    begin1()
    near0()
    pass0(0)
    far0()
    near1()
    pass0(3)
    pass0(1)
    pass1(0)
    far1()
    pass0(2)
    pass1(3)
    finish0()
    for c in outs[0]:
        c.start()
    for c in wcopies:
        c.wait()
    gate_acc[...] = first(tbuf, wg, 0)
    pass1(1)
    up_acc[...] = first(tbuf, wu, 0)
    pass1(2)
    grad_acc[...] = first(sbuf, wd, 0)
    finish1()
    for c in outs[1]:
        c.start()
    pre_gate = gate_acc[...] + first(tbuf, wg, 1)
    pre_up = up_acc[...] + first(tbuf, wu, 1)
    hidden_grad = grad_acc[...] + first(sbuf, wd, 1)
    sig = jax.nn.sigmoid(pre_gate)
    swish = pre_gate * sig
    slope = sig * (1.0 + pre_gate * (1.0 - sig))
    hid[...] = (swish * pre_up).astype(BF)
    pgg[...] = (hidden_grad * pre_up * slope).astype(BF)
    pug[...] = (hidden_grad * swish).astype(BF)

    partial = (po, pr)
    shape = (SIDE, SIDE, ROWS, Q)

    def second(h):
        def step(n, _):
            cols = pl.ds(pl.multiple_of(h * W + n * Q, Q), Q)
            to = pl.ds(pl.multiple_of(n * Q, Q), Q)
            po[h, :, :, :, to] = dot(hid[...], wd[:, cols], (1, 0)).astype(BF).reshape(shape)
            grad = dot(pgg[...], wg[:, cols], (1, 0)) + dot(pug[...], wu[:, cols], (1, 0))
            pr[h, :, :, :, to] = grad.astype(BF).reshape(shape)
            return 0

        lax.fori_loop(0, 4, step, 0)

    def cols_of(half):
        return pl.ds(half * H, H)

    def rs_steps(h):
        def group(part, ov):
            v = ups[1 - part][ov % SIDE]
            return partial[part].at[h, v] if part == 0 else partial[part].at[h, :, v]

        def piece(part, ou):
            u, v = ups[part][ou % SIDE], ups[1 - part][0]
            return partial[part].at[h, v, u] if part == 0 else partial[part].at[h, u, v]

        def rs(part, ident, src, dst, du, dv):
            return remote(
                src, dst, rs_ss.at[h, part, ident], rs_rs.at[h, part, ident], device(part, du, dv)
            )

        def far(part, d):
            src = group(part, 2).at[:, :, cols_of(d)]
            return rs(part, d, src, r1.at[h, part, d], 0, sign[d])

        def near(part, d, c):
            src = group(part, sign[d]).at[:, :, cols_of(c)]
            return rs(part, 2 + 2 * d + c, src, r2.at[h, part, d, c], 0, sign[d])

        def far_block(part, d):
            src = piece(part, 2).at[:, cols_of(d)]
            return rs(part, 6 + d, src, r3.at[h, part, d], sign[d], 0)

        def near_block(part, d, c):
            src = piece(part, sign[d]).at[:, cols_of(c)]
            return rs(part, 8 + 2 * d + c, src, r4.at[h, part, d, c], sign[d], 0)

        def begin():
            for d in range(2):
                for part in range(2):
                    go(far(part, d))
            for d in range(2):
                for part in range(2):
                    go(near(part, d, 1 - d))

        def add_far():
            for d in range(2):
                for part in range(2):
                    far(part, d).wait_recv()
                    ref = group(part, sign[d]).at[:, :, cols_of(d)]
                    ref[...] = (ref[...].astype(F32) + r1[h, part, d].astype(F32)).astype(BF)
                    go(near(part, d, d))

        def add_near():
            for part in range(2):
                for d in range(2):
                    for c in range(2):
                        near(part, d, c).wait_recv()
                for o in (2, 1, 3, 0):
                    u = ups[part][o]
                    for c in range(2):
                        ref = piece(part, o).at[:, cols_of(c)]
                        ref[...] = (
                            ref[...].astype(F32)
                            + r2[h, part, 0, c, u].astype(F32)
                            + r2[h, part, 1, c, u].astype(F32)
                        ).astype(BF)
                    if o == 2:
                        go(far_block(part, 0))
                        go(far_block(part, 1))
                    elif o != 0:
                        d = 0 if o == 1 else 1
                        go(near_block(part, d, 1 - d))

        def add_far_block():
            for part, d in both:
                far_block(part, d).wait_recv()
                ref = piece(part, sign[d]).at[:, cols_of(d)]
                ref[...] = (ref[...].astype(F32) + r3[h, part, d].astype(F32)).astype(BF)
                go(near_block(part, d, d))

        def finish():
            reduced = []
            for part in range(2):
                for c in range(2):
                    for d in range(2):
                        near_block(part, d, c).wait_recv()
                    full = (
                        piece(part, 0)[:, cols_of(c)].astype(F32)
                        + r4[h, part, 0, c].astype(F32)
                        + r4[h, part, 1, c].astype(F32)
                    ).astype(BF)
                    reduced += [full[:, :Q], full[:, Q:]]
            back = dot(fmat[...], jnp.concatenate(reduced, axis=0), (0, 0))
            esend[h] = back.astype(BF).reshape(PL, ROWS, Q)
            each(PL, lambda k: e_copy(h, k, dp).start())
            erecv[h, dp] = esend[h, dp]

        return begin, add_far, add_near, add_far_block, finish

    def to_shards(h):
        each(PL, lambda k: e_copy(h, k, at_p(PL - k)).wait_recv())
        back = dot(qmat[...], erecv[h].reshape(256, Q), (0, 0))
        zsback[h] = back.astype(BF).reshape(EXP, 32, Q)
        each(EXP, lambda k: b_copy(h, k, ex).start())
        zrback[h, ex] = zsback[h, ex]

    def at_shard(h):
        each(EXP, lambda k: b_copy(h, k, at_z(EXP - k)).wait_recv())
        zr_ref[h] = zrback[h].reshape(256, Q)

    steps = [rs_steps(h) for h in halves]
    for h in halves:
        second(h)
        steps[h][0]()
    acts = []
    for i, (src, dst) in enumerate(((hid, hid_t), (pgg, pgg_t), (pug, pug_t))):
        turned[i] = src[...].T
        acts.append(pltpu.make_async_copy(turned.at[i], dst, act_sem.at[i]))
        acts[i].start()
    steps[0][1]()
    steps[1][1]()
    steps[0][2]()
    steps[1][2]()
    steps[0][3]()
    steps[0][4]()
    steps[1][3]()
    steps[1][4]()
    for h in halves:
        to_shards(h)
    for h in halves:
        at_shard(h)

    each(EXP, lambda k: c_copy(k, ex).wait_send())
    each(PL, lambda k: l_copy(k, dp).wait_send())
    for h in halves:
        each(EXP, lambda k, h=h: z_copy(h, k, ex).wait_send())
        each(EXP, lambda k, h=h: b_copy(h, k, ex).wait_send())
        each(PL, lambda k, h=h: x_copy(h, k, dp).wait_send())
        each(PL, lambda k, h=h: e_copy(h, k, dp).wait_send())
    for c in sent:
        c.wait_send()
    for h in halves:
        for c in outs[h]:
            c.wait()
    for c in acts:
        c.wait()


def run_main(chosen, gate, counts, tokens, cotangent, wg, wu, wd):
    vmem = pl.BlockSpec(memory_space=pltpu.VMEM)
    anym = pl.BlockSpec(memory_space=pl.ANY)
    dma = pltpu.SemaphoreType.DMA

    def exchange(peers):
        return [pltpu.VMEM((HALVES, peers, 256 // peers, Q), BF)] * 2

    return pl.pallas_call(
        main_kernel,
        out_shape=(
            jax.ShapeDtypeStruct((HALVES, PL, ROWS, W), BF),
            jax.ShapeDtypeStruct((HALVES, PL, ROWS, W), BF),
            jax.ShapeDtypeStruct((HID, LIVE), BF),
            jax.ShapeDtypeStruct((HID, LIVE), BF),
            jax.ShapeDtypeStruct((HID, LIVE), BF),
            jax.ShapeDtypeStruct((HALVES, 256, Q), BF),
        ),
        in_specs=[vmem] * 3 + [pl.BlockSpec(memory_space=pltpu.SMEM)] + [anym] * 5,
        out_specs=(anym, anym, anym, anym, anym, vmem),
        scratch_shapes=[
            pltpu.VMEM((HALVES, 8, TOK, Q), BF),
            *[pltpu.VMEM((HID, D), BF)] * 3,
            pltpu.VMEM((EXP, 8, 128), jnp.int32),
            pltpu.VMEM((EXP, 8, 128), jnp.int32),
            pltpu.VMEM((8, 128), jnp.int32),
            pltpu.VMEM((PL, 8, 128), jnp.int32),
            *exchange(EXP),
            *exchange(PL),
            *exchange(PL),
            *exchange(EXP),
            *[pltpu.VMEM((HALVES, PL, ROWS, W), BF)] * 2,
            *[pltpu.VMEM((LIVE, HID), F32)] * 3,
            *[pltpu.VMEM((LIVE, HID), BF)] * 3,
            pltpu.VMEM((3, HID, LIVE), BF),
            *[pltpu.VMEM((HALVES, SIDE, SIDE, ROWS, W), BF)] * 2,
            pltpu.VMEM((HALVES, 2, 2, SIDE, ROWS, H), BF),
            pltpu.VMEM((HALVES, 2, 2, 2, SIDE, ROWS, H), BF),
            pltpu.VMEM((HALVES, 2, 2, ROWS, H), BF),
            pltpu.VMEM((HALVES, 2, 2, 2, ROWS, H), BF),
            pltpu.VMEM((256, 256), BF),
            pltpu.VMEM((128, 256), BF),
            dma((HALVES, 8)),
            dma((3,)),
            dma((HALVES, 2)),
            dma((3,)),
            *[dma((EXP,))] * 2,
            *[dma((PL,))] * 2,
            *[dma((HALVES, EXP))] * 2,
            *[dma((HALVES, PL))] * 2,
            *[dma((HALVES, PL))] * 2,
            *[dma((HALVES, EXP))] * 2,
            *[dma((HALVES, 2, 20))] * 2,
            *[dma((HALVES, 2, 12))] * 2,
        ],
        compiler_params=pltpu.CompilerParams(
            collective_id=0, has_side_effects=True, vmem_limit_bytes=58 * 1024 * 1024
        ),
        cost_estimate=pl.CostEstimate(
            flops=6 * 2 * LIVE * D * HID, bytes_accessed=20 << 20, transcendentals=LIVE * HID
        ),
        name="routed_experts",
    )(chosen, gate, counts, counts, tokens, cotangent, wg, wu, wd)


def tail_kernel(
    chosen_ref, gate_ref, cnt_ref, t_hbm, s_hbm, hid_hbm, pgg_hbm, pug_hbm, zr_hbm, cot_hbm,
    comb_out, tg_out, prob_ref, gg_out, gu_out, gd_out,
    t, s, hid, pgg, pug, zr, cot, comb, tg, gg, gu, gd, in_sem, out_sem,
):
    def load(src, dst, i):
        c = pltpu.make_async_copy(src, dst, in_sem.at[i])
        c.start()
        return c

    order = [
        [load(pgg_hbm, pgg, 0), load(t_hbm.at[0], t.at[0], 1), load(pug_hbm, pug, 2)],
        [load(hid_hbm, hid, 3), load(s_hbm.at[0], s.at[0], 4)],
        [load(zr_hbm, zr, 5), load(cot_hbm, cot, 6)],
        [load(t_hbm.at[1], t.at[1], 7), load(s_hbm.at[1], s.at[1], 8)],
    ]
    stores = []

    def store(src, dst, cols, i, n):
        c = pltpu.make_async_copy(src.at[:, cols], dst.at[:, cols], out_sem.at[i, n])
        c.start()
        stores.append(c)

    r = iota((32, EXP), 0)
    token, weight, used = of_rows(r & 7, r >> 3, chosen_ref, gate_ref, cnt_ref)
    match = iota((32, TOK), 1) == token
    pick_w = jnp.where(match, weight, F32(0.0)).astype(BF)
    pick_live = jnp.where(match, used, F32(0.0)).astype(BF)
    r = iota((64, 1), 0)
    target = ((r & 7) << 5) + ((r >> 5) << 2) + ((r >> 3) & 3)
    lane = iota((64, 256), 1)
    part = jnp.zeros((32, 128), F32)

    def wait(copies):
        for c in copies:
            c.wait()

    for n in range(D // Q):
        h, q = n // 4, n % 4
        cols = pl.ds(n * Q, Q)
        here = pl.ds(q * Q, Q)
        if n == 0:
            wait(order[0])
        elif n == 4:
            wait(order[3])
        tile = t[h, :, :, here].reshape(LIVE, Q)
        gg[:, cols] = dot(pgg[...], tile, (1, 0)).astype(BF)
        store(gg, gg_out, cols, 0, n)
        gu[:, cols] = dot(pug[...], tile, (1, 0)).astype(BF)
        store(gu, gu_out, cols, 1, n)
        if n == 0:
            wait(order[1])
        gd[:, cols] = dot(hid[...], s[h, :, :, here].reshape(LIVE, Q), (1, 0)).astype(BF)
        store(gd, gd_out, cols, 2, n)
        if n == 0:
            wait(order[2])
        pick = jnp.where(lane == target + q * 8, F32(1.0), F32(0.0)).astype(BF)
        rows = dot(pick, zr[h], (1, 0))
        out_rows = rows[:32]
        comb[:, cols] = dot(pick_w, out_rows.astype(BF), (0, 0)).astype(BF)
        store(comb, comb_out, cols, 3, n)
        tg[:, cols] = dot(pick_live, rows[32:].astype(BF), (0, 0)).astype(BF)
        store(tg, tg_out, cols, 4, n)
        prod = dot(pick_live, cot[:, cols], (1, 0)) * out_rows
        for i in range(Q // 128):
            part = part + prod[:, i * 128 : (i + 1) * 128]

    inner = jnp.sum(part, axis=1, keepdims=True)
    eye = iota((EXP, EXP), 0) == iota((EXP, EXP), 1)
    lines = [
        jnp.sum(jnp.where(eye, inner[m * EXP : (m + 1) * EXP], F32(0.0)), axis=0, keepdims=True)
        for m in range(M)
    ]
    prob_ref[...] = jnp.concatenate(lines, axis=0).astype(BF)
    wait(stores)


def run_tail(chosen, gate, counts, t, s, hid, pgg, pug, zr, cotangent):
    vmem = pl.BlockSpec(memory_space=pltpu.VMEM)
    anym = pl.BlockSpec(memory_space=pl.ANY)
    tokens = jax.ShapeDtypeStruct((TOK, D), BF)
    grads = jax.ShapeDtypeStruct((HID, D), BF)
    return pl.pallas_call(
        tail_kernel,
        out_shape=(tokens, tokens, jax.ShapeDtypeStruct((M, EXP), BF), grads, grads, grads),
        in_specs=[vmem] * 3 + [anym] * 7,
        out_specs=(anym, anym, vmem, anym, anym, anym),
        scratch_shapes=[
            *[pltpu.VMEM((HALVES, PL, ROWS, W), BF)] * 2,
            *[pltpu.VMEM((HID, LIVE), BF)] * 3,
            pltpu.VMEM((HALVES, 256, Q), BF),
            *[pltpu.VMEM((TOK, D), BF)] * 3,
            *[pltpu.VMEM((HID, D), BF)] * 3,
            pltpu.SemaphoreType.DMA((9,)),
            pltpu.SemaphoreType.DMA((5, D // Q)),
        ],
        compiler_params=pltpu.CompilerParams(vmem_limit_bytes=58 * 1024 * 1024),
        cost_estimate=pl.CostEstimate(
            flops=3 * 2 * LIVE * D * HID, bytes_accessed=20 << 20, transcendentals=0
        ),
        name="weight_grads_and_combine",
    )(chosen, gate, counts, t, s, hid, pgg, pug, zr, cotangent)


def per_device(tokens, cotangent, chosen, counts, gate_prob, w_gate, w_up, w_down):
    routes = (chosen[0].T, gate_prob[0].T, counts)
    t, s, hid, pgg, pug, zr = run_main(
        *routes, tokens, cotangent, w_gate[0].T, w_up[0].T, w_down[0]
    )
    combined, token_grad, prob_grad, gg, gu, gd = run_tail(
        *routes, t, s, hid, pgg, pug, zr, cotangent
    )
    return combined, token_grad, prob_grad.T[None], gg.T[None], gu.T[None], gd[None]


def solution(mesh):
    tokens = P(("dp", "expert"), None)
    slots = P(("dp", "expert"), None, None)
    specs = (tokens, tokens, slots, tokens, slots)
    weights = (P("expert", None, "dp"), P("expert", None, "dp"), P("expert", "dp", None))
    return jax.shard_map(
        per_device,
        mesh=mesh,
        in_specs=specs + weights,
        out_specs=(tokens, tokens, slots) + weights,
        check_vma=False,
    )
```

```python
import functools

import jax
import jax.numpy as jnp
from jax import lax
from jax.experimental import pallas as pl
from jax.experimental.pallas import tpu as pltpu
from jax.sharding import PartitionSpec as P

MESH = pl.DeviceIdType.MESH
BF = jnp.bfloat16
F32 = jnp.float32

D = 4096
HID = 448
TOK = 128
EXP = 8
PL = 16
SIDE = 4
M = 4
ROWS = 16
LIVE = ROWS * PL
CHUNKS = 2
W = D // CHUNKS
TILE = 512
AG_LAG, RS_LAG = 2, 1
Q = W // 4
H = W // 2


def interleave(chunks, lag, newest_first):
    count = len(chunks[0]) + lag * (len(chunks) - 1)
    for t in range(count):
        for c in reversed(range(len(chunks))) if newest_first else range(len(chunks)):
            if 0 <= t - lag * c < len(chunks[c]):
                chunks[c][t - lag * c]()


def dot(a, b, contract):
    return lax.dot_general(
        a, b, (((contract[0],), (contract[1],)), ((), ())), preferred_element_type=F32
    )


def iota(shape, dim):
    return lax.broadcasted_iota(jnp.int32, shape, dim)


def of_rows(expert, m, chosen_ref, gate_ref, cnt_ref):
    chosen = jnp.zeros(m.shape, F32)
    gate = jnp.zeros(m.shape, F32)
    for i in range(M):
        chosen = jnp.where(m == i, chosen_ref[i : i + 1, :].astype(F32), chosen)
        gate = jnp.where(m == i, gate_ref[i : i + 1, :].astype(F32), gate)
    here = iota(m.shape, 1) == expert
    live = here & (m < cnt_ref[...])

    def take(v, mask):
        return jnp.sum(jnp.where(mask, v, F32(0.0)), axis=1, keepdims=True)

    return take(chosen, here).astype(jnp.int32), take(gate, live), take(F32(1.0), live)


def main_kernel(
    chosen_ref, gate_ref, cnt_ref, cnt_smem, tok_hbm, cot_hbm, wg_hbm, wu_hbm, wd_hbm,
    t_out, s_out, hid_t, pgg_t, pug_t, zr_out,
    x_in, wg, wu, wd, csend, crecv, lsend, lrecv,
    zsend, zrecv, xsend, xrecv, esend, erecv, zsback,
    tbuf, sbuf, gate_acc, up_acc, grad_acc, hid, pgg, pug, turned, po, pr, r1, r2, r3, r4, qmat, fmat,
    in_sem, w_sem, out_sem, act_sem, keep_sem, c_ss, c_rs, l_ss, l_rs, z_ss, z_rs, x_ss, x_rs,
    e_ss, e_rs, b_ss, b_rs, ag_ss, ag_rs, rs_ss, rs_rs,
):
    dp = lax.axis_index("dp")
    ex = lax.axis_index("expert")
    x, y = lax.rem(dp, SIDE), lax.div(dp, SIDE)
    chunks = range(CHUNKS)

    def at_z(k):
        return lax.rem(ex + k, EXP)

    def at_p(k):
        return lax.rem(dp + k, PL)

    def each(count, body):
        def step(k, _):
            body(k)
            return 0

        lax.fori_loop(1, count, step, 0)

    loads = [
        [
            pltpu.make_async_copy(
                src.at[:, pl.ds(h * W + q * Q, Q)], x_in.at[h, a * 4 + q], in_sem.at[h, a * 4 + q]
            )
            for a, src in enumerate((tok_hbm, cot_hbm))
            for q in range(4)
        ]
        for h in chunks
    ]
    for h in chunks:
        for c in loads[h]:
            c.start()
    barrier = pltpu.get_barrier_semaphore()

    def greet(device):
        pl.semaphore_signal(barrier, inc=1, device_id=device, device_id_type=MESH)

    each(EXP, lambda k: greet((dp, at_z(k))))
    each(PL, lambda k: greet((at_p(k), ex)))
    wcopies = [
        pltpu.make_async_copy(src, dst, w_sem.at[i])
        for i, (src, dst) in enumerate(((wg_hbm, wg), (wu_hbm, wu), (wd_hbm, wd)))
    ]

    for e in range(EXP):
        csend[e] = jnp.full((8, 128), cnt_smem[0, e], jnp.int32)
    r = iota((256, EXP), 0)
    token, weight, _ = of_rows(r >> 5, r & 3, chosen_ref, gate_ref, cnt_ref)
    r = iota((256, 1), 0)
    token = token + (((r >> 2) & 1) * 4 + ((r >> 3) & 3)) * TOK
    weight = jnp.where((r & 4) == 0, F32(1.0), weight)
    pick = jnp.where(iota((256, 8 * TOK), 1) == token, weight, F32(0.0)).astype(BF)

    def remote(src, dst, ss, rs, device):
        return pltpu.make_async_remote_copy(
            src_ref=src, dst_ref=dst, send_sem=ss, recv_sem=rs, device_id=device,
            device_id_type=MESH,
        )

    def c_copy(k, dst):
        return remote(csend.at[at_z(k)], crecv.at[dst], c_ss.at[k], c_rs.at[k], (dp, at_z(k)))

    def z_copy(h, k, dst):
        return remote(
            zsend.at[h, at_z(k)], zrecv.at[h, dst], z_ss.at[h, k], z_rs.at[h, k], (dp, at_z(k))
        )

    def b_copy(h, k, dst):
        return remote(
            zsback.at[h, at_z(k)], zr_out.at[h, dst], b_ss.at[h, k], b_rs.at[h, k], (dp, at_z(k))
        )

    def keep(h):
        return pltpu.make_async_copy(zsback.at[h, ex], zr_out.at[h, ex], keep_sem.at[h])

    def l_copy(k, dst):
        return remote(lsend, lrecv.at[dst], l_ss.at[k], l_rs.at[k], (at_p(k), ex))

    def x_copy(h, k, dst):
        return remote(
            xsend.at[h, at_p(k)], xrecv.at[h, dst], x_ss.at[h, k], x_rs.at[h, k], (at_p(k), ex)
        )

    def e_copy(h, k, dst):
        return remote(
            esend.at[h, at_p(k)], erecv.at[h, dst], e_ss.at[h, k], e_rs.at[h, k], (at_p(k), ex)
        )

    for h in chunks:
        for c in loads[h]:
            c.wait()
        if h == CHUNKS - 1:
            for c in wcopies:
                c.start()
        zsend[h] = dot(pick, x_in[h].reshape(8 * TOK, Q), (1, 0)).astype(BF).reshape(EXP, 32, Q)
        if h == 0:
            pl.semaphore_wait(barrier, EXP - 1 + PL - 1)
            each(EXP, lambda k: c_copy(k, ex).start())
        each(EXP, lambda k, h=h: z_copy(h, k, ex).start())
        zrecv[h, ex] = zsend[h, ex]
    crecv[ex] = csend[ex]
    each(EXP, lambda k: c_copy(k, at_z(EXP - k)).wait_recv())

    total = crecv[0]
    for s in range(1, EXP):
        total = total + crecv[s]
    lsend[...] = total
    lrecv[dp] = total
    each(PL, lambda k: l_copy(k, dp).start())

    lane = iota((8, 256), 1)
    src = lane >> 5
    rank = lane & 3
    used = jnp.zeros((8, 256), jnp.int32)
    for s in range(EXP):
        v = jnp.concatenate([crecv[s], crecv[s]], axis=1)
        used = jnp.where(src == s, v, used)
        if s < EXP - 1:
            rank = rank + jnp.where(src > s, v, 0)
    alive = (lane & 3) < used

    each(PL, lambda k: l_copy(k, at_p(PL - k)).wait_recv())
    zero = jnp.zeros((8, 128), jnp.int32)
    before = zero
    col = lane >> 4
    off_l = jnp.zeros((8, 256), jnp.int32)
    len_l = jnp.zeros((8, 256), jnp.int32)
    running = zero
    for i in range(PL):
        v = lrecv[i]
        off_l = jnp.where(col == i, jnp.concatenate([running, running], axis=1), off_l)
        len_l = jnp.where(col == i, jnp.concatenate([v, v], axis=1), len_l)
        before = before + jnp.where(i < dp, v, zero)
        running = running + v
    dealt = rank + jnp.concatenate([before, before], axis=1)
    to = ((dealt & 15) << 4) + (((lane >> 3) & 3) << 2) + (((lane >> 2) & 1) << 1) + (rank >> 4)
    to = jnp.where(alive, to, -1)[0:1, :]
    qmat[...] = jnp.where(iota((256, 256), 0) == to, F32(1.0), F32(0.0)).astype(BF)
    own = ((dp - off_l + 512) & 15) + ((lane & 1) << 4)
    to = (((lane >> 1) & 1) << 6) + (((lane >> 2) & 3) << 4) + ((off_l + own) >> 4)
    to = jnp.where(own < len_l, to, -1)[0:1, :]
    fmat[...] = jnp.where(iota((128, 256), 0) == to, F32(1.0), F32(0.0)).astype(BF)

    for h in chunks:
        each(EXP, lambda k, h=h: z_copy(h, k, at_z(EXP - k)).wait_recv())
        xsend[h] = (
            dot(qmat[...], zrecv[h].reshape(256, Q), (1, 0)).astype(BF).reshape(PL, ROWS, Q)
        )
        each(PL, lambda k, h=h: x_copy(h, k, dp).start())
        xrecv[h, dp] = xsend[h, dp]

    def compact(h):
        each(PL, lambda k: x_copy(h, k, at_p(PL - k)).wait_recv())
        mine = dot(fmat[...], xrecv[h].reshape(256, Q), (1, 0)).astype(BF)
        for q in range(4):
            tbuf[h, dp, :, pl.ds(q * Q, Q)] = mine[q * 16 : q * 16 + 16]
            sbuf[h, dp, :, pl.ds(q * Q, Q)] = mine[64 + q * 16 : 64 + q * 16 + 16]

    ups = [[lax.rem(v + o, SIDE) if o else v for o in range(SIDE)] for v in (x, y)]
    blocks = [[ups[1][oy] * SIDE + ups[0][ox] for ox in range(SIDE)] for oy in range(SIDE)]

    def block_of(part, ou, ov):
        ou, ov = ou % SIDE, ov % SIDE
        return blocks[ov][ou] if part == 0 else blocks[ou][ov]

    def device(part, du, dv):
        return (block_of(part, du, dv), ex)

    gathered = (tbuf, sbuf)
    sign = (1, -1)
    both = [(part, d) for part in range(2) for d in range(2)]
    sent = []

    def go(c):
        c.start()
        sent.append(c)

    def ag_steps(h):
        def ag(part, ident, block, half, du, dv):
            ref = gathered[part].at[h, block]
            if half is not None:
                ref = ref.at[:, pl.ds(half * H, H)]
            return remote(
                ref, ref, ag_ss.at[h, part, ident], ag_rs.at[h, part, ident], device(part, du, dv)
            )

        def phase2(part, o):
            for d in range(2):
                go(ag(part, 4 + o * 4 + d, block_of(part, o, 0), None, 0, sign[d]))

        def begin():
            for part, d in both:
                go(ag(part, d, block_of(part, 0, 0), None, sign[d], 0))
            for part in range(2):
                phase2(part, 0)

        def near():
            for part, d in both:
                o = 3 if d == 0 else 1
                b = block_of(part, o, 0)
                ag(part, d, b, None, sign[d], 0).wait_recv()
                go(ag(part, 2 + d, b, d, sign[d], 0))
            for part, d in both:
                phase2(part, 3 if d == 0 else 1)

        def far():
            for part, d in both:
                ag(part, 2 + d, block_of(part, 2, 0), d, sign[d], 0).wait_recv()
            for part in range(2):
                phase2(part, 2)

        def pass_on(o):
            for part, d in both:
                b = block_of(part, o, -sign[d])
                ag(part, 4 + o * 4 + d, b, None, 0, sign[d]).wait_recv()
                go(ag(part, 4 + o * 4 + 2 + d, b, d, 0, sign[d]))

        def finish():
            for o in (0, 3, 1, 2):
                for part, d in both:
                    b = block_of(part, o, 2)
                    ag(part, 4 + o * 4 + 2 + d, b, d, 0, sign[d]).wait_recv()

        return begin, near, far, pass_on, finish

    outs = [
        [
            pltpu.make_async_copy(buf.at[h], out.at[h], out_sem.at[h, i])
            for i, (buf, out) in enumerate(((tbuf, t_out), (sbuf, s_out)))
        ]
        for h in chunks
    ]

    def first(buf, w, h):
        return dot(buf[h].reshape(LIVE, W), w[:, pl.ds(h * W, W)], (1, 1))

    def gather_steps(h):
        begin, near, far, pass_on, finish = ag_steps(h)

        def start():
            compact(h)
            begin()

        def end():
            finish()
            for c in outs[h]:
                c.start()
            if h == 0:
                for c in wcopies:
                    c.wait()

        def add(acc, buf, w):
            acc[...] = first(buf, w, h) if h == 0 else acc[...] + first(buf, w, h)

        return [
            start,
            near,
            lambda: pass_on(0),
            far,
            lambda: pass_on(3),
            lambda: pass_on(1),
            lambda: pass_on(2),
            end,
            lambda: add(gate_acc, tbuf, wg),
            lambda: add(up_acc, tbuf, wu),
            lambda: add(grad_acc, sbuf, wd) if h < CHUNKS - 1 else None,
        ]

    interleave([gather_steps(h) for h in chunks], AG_LAG, False)
    pre_gate = gate_acc[...]
    pre_up = up_acc[...]
    sig = jax.nn.sigmoid(pre_gate)
    swish = pre_gate * sig
    hid[...] = (swish * pre_up).astype(BF)
    gate_acc[...] = swish
    up_acc[...] = pre_up * (sig * (1.0 + pre_gate * (1.0 - sig)))

    def hidden_grads():
        hidden_grad = grad_acc[...] + first(sbuf, wd, CHUNKS - 1)
        pgg[...] = (hidden_grad * up_acc[...]).astype(BF)
        pug[...] = (hidden_grad * gate_acc[...]).astype(BF)

    partial = (po, pr)
    shape = (SIDE, SIDE, ROWS, TILE)

    def second(h, part, half):
        def step(n, _):
            cols = pl.ds(pl.multiple_of(h * W + n * TILE, TILE), TILE)
            to = pl.ds(pl.multiple_of(n * TILE, TILE), TILE)
            if part == 0:
                sums = dot(hid[...], wd[:, cols], (1, 0))
            else:
                sums = dot(pgg[...], wg[:, cols], (1, 0)) + dot(pug[...], wu[:, cols], (1, 0))
            partial[part][h, :, :, :, to] = sums.astype(BF).reshape(shape)
            return 0

        lax.fori_loop(half * H // TILE, (half + 1) * H // TILE, step, 0)

    def cols_of(half):
        return pl.ds(half * H, H)

    def rs_steps(h):
        def group(part, ov):
            v = ups[1 - part][ov % SIDE]
            return partial[part].at[h, v] if part == 0 else partial[part].at[h, :, v]

        def piece(part, ou):
            u, v = ups[part][ou % SIDE], ups[1 - part][0]
            return partial[part].at[h, v, u] if part == 0 else partial[part].at[h, u, v]

        def rs(part, ident, src, dst, du, dv):
            return remote(
                src, dst, rs_ss.at[h, part, ident], rs_rs.at[h, part, ident], device(part, du, dv)
            )

        def far(part, d):
            src = group(part, 2).at[:, :, cols_of(d)]
            return rs(part, d, src, r1.at[h, part, d], 0, sign[d])

        def near(part, d, c):
            src = group(part, sign[d]).at[:, :, cols_of(c)]
            return rs(part, 2 + 2 * d + c, src, r2.at[h, part, d, c], 0, sign[d])

        def far_block(part):
            src = piece(part, 2)
            return rs(part, 6, src, r3.at[h, part], 2, 0)

        def near_block(part, d):
            src = piece(part, sign[d])
            return rs(part, 7 + d, src, r4.at[h, part, d], sign[d], 0)

        def begin(part):
            for c in range(2):
                second(h, part, c)
                go(far(part, c))
                go(near(part, 1 - c, c))

        def add_far():
            for d in range(2):
                for part in range(2):
                    far(part, d).wait_recv()
                    ref = group(part, sign[d]).at[:, :, cols_of(d)]
                    ref[...] = (ref[...].astype(F32) + r1[h, part, d].astype(F32)).astype(BF)
                    go(near(part, d, d))

        def add_near():
            for part in range(2):
                for d in range(2):
                    for c in range(2):
                        near(part, d, c).wait_recv()
                for o in (2, 1, 3, 0):
                    u = ups[part][o]
                    for c in range(2):
                        ref = piece(part, o).at[:, cols_of(c)]
                        ref[...] = (
                            ref[...].astype(F32)
                            + r2[h, part, 0, c, u].astype(F32)
                            + r2[h, part, 1, c, u].astype(F32)
                        ).astype(BF)
                    if o == 2:
                        go(far_block(part))
                    elif o != 0:
                        go(near_block(part, 0 if o == 1 else 1))

        def finish():
            reduced = []
            for part in range(2):
                for d in range(2):
                    near_block(part, d).wait_recv()
                far_block(part).wait_recv()
                for q in range(4):
                    cols = pl.ds(q * Q, Q)
                    reduced.append(
                        (
                            piece(part, 0)[:, cols].astype(F32)
                            + r4[h, part, 0, :, cols].astype(F32)
                            + r4[h, part, 1, :, cols].astype(F32)
                            + r3[h, part, :, cols].astype(F32)
                        ).astype(BF)
                    )
            back = dot(fmat[...], jnp.concatenate(reduced, axis=0), (0, 0))
            esend[h] = back.astype(BF).reshape(PL, ROWS, Q)
            each(PL, lambda k: e_copy(h, k, dp).start())
            erecv[h, dp] = esend[h, dp]

        return begin, add_far, add_near, finish

    def to_shards(h):
        each(PL, lambda k: e_copy(h, k, at_p(PL - k)).wait_recv())
        back = dot(qmat[...], erecv[h].reshape(256, Q), (0, 0))
        zsback[h] = back.astype(BF).reshape(EXP, 32, Q)
        each(EXP, lambda k: b_copy(h, k, ex).start())
        keep(h).start()

    def at_shard(h):
        each(EXP, lambda k: b_copy(h, k, at_z(EXP - k)).wait_recv())
        keep(h).wait()

    acts = []

    def turn():
        for i, (src, dst) in enumerate(((hid, hid_t), (pgg, pgg_t), (pug, pug_t))):
            turned[i] = src[...].T
            acts.append(pltpu.make_async_copy(turned.at[i], dst, act_sem.at[i]))
            acts[i].start()

    def reduce_steps(h):
        begin, add_far, add_near, finish = rs_steps(h)

        def start():
            begin(0)
            if h == 0:
                hidden_grads()
            begin(1)
            if h == CHUNKS - 1:
                turn()

        return [
            start,
            add_far,
            add_near,
            finish,
            lambda: to_shards(h),
            lambda: at_shard(h),
        ]

    interleave([reduce_steps(h) for h in chunks], RS_LAG, True)

    each(EXP, lambda k: c_copy(k, ex).wait_send())
    each(PL, lambda k: l_copy(k, dp).wait_send())
    for h in chunks:
        each(EXP, lambda k, h=h: z_copy(h, k, ex).wait_send())
        each(EXP, lambda k, h=h: b_copy(h, k, ex).wait_send())
        each(PL, lambda k, h=h: x_copy(h, k, dp).wait_send())
        each(PL, lambda k, h=h: e_copy(h, k, dp).wait_send())
    for c in sent:
        c.wait_send()
    for h in chunks:
        for c in outs[h]:
            c.wait()
    for c in acts:
        c.wait()


def run_main(chosen, gate, counts, tokens, cotangent, wg, wu, wd):
    vmem = pl.BlockSpec(memory_space=pltpu.VMEM)
    anym = pl.BlockSpec(memory_space=pl.ANY)
    dma = pltpu.SemaphoreType.DMA

    def exchange(peers):
        return [pltpu.VMEM((CHUNKS, peers, 256 // peers, Q), BF)] * 2

    return pl.pallas_call(
        main_kernel,
        out_shape=(
            jax.ShapeDtypeStruct((CHUNKS, PL, ROWS, W), BF),
            jax.ShapeDtypeStruct((CHUNKS, PL, ROWS, W), BF),
            jax.ShapeDtypeStruct((HID, LIVE), BF),
            jax.ShapeDtypeStruct((HID, LIVE), BF),
            jax.ShapeDtypeStruct((HID, LIVE), BF),
            jax.ShapeDtypeStruct((CHUNKS, EXP, 32, Q), BF),
        ),
        in_specs=[vmem] * 3 + [pl.BlockSpec(memory_space=pltpu.SMEM)] + [anym] * 5,
        out_specs=(anym,) * 6,
        scratch_shapes=[
            pltpu.VMEM((CHUNKS, 8, TOK, Q), BF),
            *[pltpu.VMEM((HID, D), BF)] * 3,
            pltpu.VMEM((EXP, 8, 128), jnp.int32),
            pltpu.VMEM((EXP, 8, 128), jnp.int32),
            pltpu.VMEM((8, 128), jnp.int32),
            pltpu.VMEM((PL, 8, 128), jnp.int32),
            *exchange(EXP),
            *exchange(PL),
            *exchange(PL),
            exchange(EXP)[0],
            *[pltpu.VMEM((CHUNKS, PL, ROWS, W), BF)] * 2,
            *[pltpu.VMEM((LIVE, HID), F32)] * 3,
            *[pltpu.VMEM((LIVE, HID), BF)] * 3,
            pltpu.VMEM((3, HID, LIVE), BF),
            *[pltpu.VMEM((CHUNKS, SIDE, SIDE, ROWS, W), BF)] * 2,
            pltpu.VMEM((CHUNKS, 2, 2, SIDE, ROWS, H), BF),
            pltpu.VMEM((CHUNKS, 2, 2, 2, SIDE, ROWS, H), BF),
            pltpu.VMEM((CHUNKS, 2, ROWS, W), BF),
            pltpu.VMEM((CHUNKS, 2, 2, ROWS, W), BF),
            pltpu.VMEM((256, 256), BF),
            pltpu.VMEM((128, 256), BF),
            dma((CHUNKS, 8)),
            dma((3,)),
            dma((CHUNKS, 2)),
            dma((3,)),
            dma((CHUNKS,)),
            *[dma((EXP,))] * 2,
            *[dma((PL,))] * 2,
            *[dma((CHUNKS, EXP))] * 2,
            *[dma((CHUNKS, PL))] * 2,
            *[dma((CHUNKS, PL))] * 2,
            *[dma((CHUNKS, EXP))] * 2,
            *[dma((CHUNKS, 2, 20))] * 2,
            *[dma((CHUNKS, 2, 9))] * 2,
        ],
        compiler_params=pltpu.CompilerParams(
            collective_id=0, has_side_effects=True, vmem_limit_bytes=58 * 1024 * 1024
        ),
        cost_estimate=pl.CostEstimate(
            flops=6 * 2 * LIVE * D * HID, bytes_accessed=20 << 20, transcendentals=LIVE * HID
        ),
        name="routed_experts",
    )(chosen, gate, counts, counts, tokens, cotangent, wg, wu, wd)


def tail_kernel(
    chosen_ref, gate_ref, cnt_ref, t_hbm, s_hbm, hid_hbm, pgg_hbm, pug_hbm, zr_hbm, cot_hbm,
    comb_out, tg_out, prob_ref, gg_out, gu_out, gd_out,
    t, s, hid, pgg, pug, zr, cot, comb, tg, gg, gu, gd, in_sem, out_sem,
):
    def load(src, dst, i):
        c = pltpu.make_async_copy(src, dst, in_sem.at[i])
        c.start()
        return c

    order = [
        [load(pgg_hbm, pgg, 0), load(t_hbm.at[0], t.at[0], 1), load(pug_hbm, pug, 2)],
        [load(hid_hbm, hid, 3), load(s_hbm.at[0], s.at[0], 4)],
        [load(zr_hbm, zr, 5), load(cot_hbm, cot, 6)],
    ]
    later = [
        [load(t_hbm.at[h], t.at[h], 5 + 2 * h), load(s_hbm.at[h], s.at[h], 6 + 2 * h)]
        for h in range(1, CHUNKS)
    ]
    stores = []

    def store(src, dst, cols, i, n):
        c = pltpu.make_async_copy(src.at[:, cols], dst.at[:, cols], out_sem.at[i, n])
        c.start()
        stores.append(c)

    r = iota((32, EXP), 0)
    token, weight, used = of_rows(r & 7, r >> 3, chosen_ref, gate_ref, cnt_ref)
    match = iota((32, TOK), 1) == token
    pick_w = jnp.where(match, weight, F32(0.0)).astype(BF)
    pick_live = jnp.where(match, used, F32(0.0)).astype(BF)
    r = iota((64, 1), 0)
    target = ((r & 7) << 5) + ((r >> 5) << 2) + ((r >> 3) & 3)
    lane = iota((64, 256), 1)
    part = jnp.zeros((32, 128), F32)

    def wait(copies):
        for c in copies:
            c.wait()

    for n in range(D // TILE):
        h, at = n * TILE // W, n * TILE % W
        cols = pl.ds(n * TILE, TILE)
        here = pl.ds(at, TILE)
        if n == 0:
            wait(order[0])
        elif at == 0:
            wait(later[h - 1])
        tile = t[h, :, :, here].reshape(LIVE, TILE)
        gg[:, cols] = dot(pgg[...], tile, (1, 0)).astype(BF)
        store(gg, gg_out, cols, 0, n)
        gu[:, cols] = dot(pug[...], tile, (1, 0)).astype(BF)
        store(gu, gu_out, cols, 1, n)
        if n == 0:
            wait(order[1])
        gd[:, cols] = dot(hid[...], s[h, :, :, here].reshape(LIVE, TILE), (1, 0)).astype(BF)
        store(gd, gd_out, cols, 2, n)
        if n == 0:
            wait(order[2])
        pieces = []
        for q in range(at // Q, (at + TILE) // Q):
            pick = jnp.where(lane == target + q * 8, F32(1.0), F32(0.0)).astype(BF)
            pieces.append(dot(pick, zr[h], (1, 0)))
        rows = jnp.concatenate(pieces, axis=1) if len(pieces) > 1 else pieces[0]
        out_rows = rows[:32]
        comb[:, cols] = dot(pick_w, out_rows.astype(BF), (0, 0)).astype(BF)
        store(comb, comb_out, cols, 3, n)
        tg[:, cols] = dot(pick_live, rows[32:].astype(BF), (0, 0)).astype(BF)
        store(tg, tg_out, cols, 4, n)
        prod = dot(pick_live, cot[:, cols], (1, 0)) * out_rows
        for i in range(TILE // 128):
            part = part + prod[:, i * 128 : (i + 1) * 128]

    inner = jnp.sum(part, axis=1, keepdims=True)
    eye = iota((EXP, EXP), 0) == iota((EXP, EXP), 1)
    lines = [
        jnp.sum(jnp.where(eye, inner[m * EXP : (m + 1) * EXP], F32(0.0)), axis=0, keepdims=True)
        for m in range(M)
    ]
    prob_ref[...] = jnp.concatenate(lines, axis=0).astype(BF)
    wait(stores)


def run_tail(chosen, gate, counts, t, s, hid, pgg, pug, zr, cotangent):
    vmem = pl.BlockSpec(memory_space=pltpu.VMEM)
    anym = pl.BlockSpec(memory_space=pl.ANY)
    tokens = jax.ShapeDtypeStruct((TOK, D), BF)
    grads = jax.ShapeDtypeStruct((HID, D), BF)
    return pl.pallas_call(
        tail_kernel,
        out_shape=(tokens, tokens, jax.ShapeDtypeStruct((M, EXP), BF), grads, grads, grads),
        in_specs=[vmem] * 3 + [anym] * 7,
        out_specs=(anym, anym, vmem, anym, anym, anym),
        scratch_shapes=[
            *[pltpu.VMEM((CHUNKS, PL, ROWS, W), BF)] * 2,
            *[pltpu.VMEM((HID, LIVE), BF)] * 3,
            pltpu.VMEM((CHUNKS, 256, Q), BF),
            *[pltpu.VMEM((TOK, D), BF)] * 3,
            *[pltpu.VMEM((HID, D), BF)] * 3,
            pltpu.SemaphoreType.DMA((5 + 2 * CHUNKS,)),
            pltpu.SemaphoreType.DMA((5, D // TILE)),
        ],
        compiler_params=pltpu.CompilerParams(vmem_limit_bytes=58 * 1024 * 1024),
        cost_estimate=pl.CostEstimate(
            flops=3 * 2 * LIVE * D * HID, bytes_accessed=20 << 20, transcendentals=0
        ),
        name="weight_grads_and_combine",
    )(chosen, gate, counts, t, s, hid, pgg, pug, zr, cotangent)


def per_device(tokens, cotangent, chosen, counts, gate_prob, w_gate, w_up, w_down):
    routes = (chosen[0].T, gate_prob[0].T, counts)
    t, s, hid, pgg, pug, zr = run_main(
        *routes, tokens, cotangent, w_gate[0].T, w_up[0].T, w_down[0]
    )
    combined, token_grad, prob_grad, gg, gu, gd = run_tail(
        *routes, t, s, hid, pgg, pug, zr.reshape(CHUNKS, 256, Q), cotangent
    )
    return combined, token_grad, prob_grad.T[None], gg.T[None], gu.T[None], gd[None]


def solution(mesh):
    tokens = P(("dp", "expert"), None)
    slots = P(("dp", "expert"), None, None)
    specs = (tokens, tokens, slots, tokens, slots)
    weights = (P("expert", None, "dp"), P("expert", None, "dp"), P("expert", "dp", None))
    return jax.shard_map(
        per_device,
        mesh=mesh,
        in_specs=specs + weights,
        out_specs=(tokens, tokens, slots) + weights,
        check_vma=False,
    )
```

```python
import functools

import jax
import jax.numpy as jnp
from jax import lax
from jax.experimental import pallas as pl
from jax.experimental.pallas import tpu as pltpu
from jax.sharding import PartitionSpec as P

MESH = pl.DeviceIdType.MESH
BF = jnp.bfloat16
F32 = jnp.float32

D = 4096
HID = 448
TOK = 128
EXP = 8
PL = 16
SIDE = 4
M = 4
ROWS = 16
LIVE = ROWS * PL
CHUNKS = 2
W = D // CHUNKS
TILE = 512
AG_LAG, RS_LAG = 3, 1
Q = W // 4
H = W // 2


def interleave(chunks, lag, newest_first):
    count = len(chunks[0]) + lag * (len(chunks) - 1)
    for t in range(count):
        for c in reversed(range(len(chunks))) if newest_first else range(len(chunks)):
            if 0 <= t - lag * c < len(chunks[c]):
                chunks[c][t - lag * c]()


def dot(a, b, contract):
    return lax.dot_general(
        a, b, (((contract[0],), (contract[1],)), ((), ())), preferred_element_type=F32
    )


def iota(shape, dim):
    return lax.broadcasted_iota(jnp.int32, shape, dim)


def of_rows(expert, m, chosen_ref, gate_ref, cnt_ref):
    chosen = jnp.zeros(m.shape, F32)
    gate = jnp.zeros(m.shape, F32)
    for i in range(M):
        chosen = jnp.where(m == i, chosen_ref[i : i + 1, :].astype(F32), chosen)
        gate = jnp.where(m == i, gate_ref[i : i + 1, :].astype(F32), gate)
    here = iota(m.shape, 1) == expert
    live = here & (m < cnt_ref[...])

    def take(v, mask):
        return jnp.sum(jnp.where(mask, v, F32(0.0)), axis=1, keepdims=True)

    return take(chosen, here).astype(jnp.int32), take(gate, live), take(F32(1.0), live)


def main_kernel(
    chosen_ref, gate_ref, cnt_ref, cnt_smem, tok_hbm, cot_hbm, wg_hbm, wu_hbm, wd_hbm,
    t_out, s_out, hid_t, pgg_t, pug_t, zr_out,
    x_in, wg, wu, wd, csend, crecv, lsend, lrecv,
    zsend, zrecv, xsend, xrecv, esend, erecv, zsback,
    tbuf, sbuf, gate_acc, up_acc, grad_acc, hid, pgg, pug, turned, po, pr, r1, r2, r3, r4, qmat, fmat,
    in_sem, w_sem, out_sem, act_sem, keep_sem, c_ss, c_rs, l_ss, l_rs, z_ss, z_rs, x_ss, x_rs,
    e_ss, e_rs, b_ss, b_rs, ag_ss, ag_rs, rs_ss, rs_rs,
):
    dp = lax.axis_index("dp")
    ex = lax.axis_index("expert")
    x, y = lax.rem(dp, SIDE), lax.div(dp, SIDE)
    chunks = range(CHUNKS)

    def at_z(k):
        return lax.rem(ex + k, EXP)

    def at_p(k):
        return lax.rem(dp + k, PL)

    def each(count, body):
        def step(k, _):
            body(k)
            return 0

        lax.fori_loop(1, count, step, 0)

    loads = [
        [
            pltpu.make_async_copy(
                src.at[:, pl.ds(h * W + q * Q, Q)], x_in.at[h, a * 4 + q], in_sem.at[h, a * 4 + q]
            )
            for a, src in enumerate((tok_hbm, cot_hbm))
            for q in range(4)
        ]
        for h in chunks
    ]
    for h in chunks:
        for c in loads[h]:
            c.start()
    barrier = pltpu.get_barrier_semaphore()

    def greet(device):
        pl.semaphore_signal(barrier, inc=1, device_id=device, device_id_type=MESH)

    each(EXP, lambda k: greet((dp, at_z(k))))
    each(PL, lambda k: greet((at_p(k), ex)))
    wcopies = [
        pltpu.make_async_copy(src, dst, w_sem.at[i])
        for i, (src, dst) in enumerate(((wg_hbm, wg), (wu_hbm, wu), (wd_hbm, wd)))
    ]

    for e in range(EXP):
        csend[e] = jnp.full((8, 128), cnt_smem[0, e], jnp.int32)
    r = iota((256, EXP), 0)
    token, weight, _ = of_rows(r >> 5, r & 3, chosen_ref, gate_ref, cnt_ref)
    r = iota((256, 1), 0)
    token = token + (((r >> 2) & 1) * 4 + ((r >> 3) & 3)) * TOK
    weight = jnp.where((r & 4) == 0, F32(1.0), weight)
    pick = jnp.where(iota((256, 8 * TOK), 1) == token, weight, F32(0.0)).astype(BF)

    def remote(src, dst, ss, rs, device):
        return pltpu.make_async_remote_copy(
            src_ref=src, dst_ref=dst, send_sem=ss, recv_sem=rs, device_id=device,
            device_id_type=MESH,
        )

    def c_copy(k, dst):
        return remote(csend.at[at_z(k)], crecv.at[dst], c_ss.at[k], c_rs.at[k], (dp, at_z(k)))

    def z_copy(h, k, dst):
        return remote(
            zsend.at[h, at_z(k)], zrecv.at[h, dst], z_ss.at[h, k], z_rs.at[h, k], (dp, at_z(k))
        )

    def b_copy(h, k, dst):
        return remote(
            zsback.at[h, at_z(k)], zr_out.at[h, dst], b_ss.at[h, k], b_rs.at[h, k], (dp, at_z(k))
        )

    def keep(h):
        return pltpu.make_async_copy(zsback.at[h, ex], zr_out.at[h, ex], keep_sem.at[h])

    def l_copy(k, dst):
        return remote(lsend, lrecv.at[dst], l_ss.at[k], l_rs.at[k], (at_p(k), ex))

    def x_copy(h, k, dst):
        return remote(
            xsend.at[h, at_p(k)], xrecv.at[h, dst], x_ss.at[h, k], x_rs.at[h, k], (at_p(k), ex)
        )

    def e_copy(h, k, dst):
        return remote(
            esend.at[h, at_p(k)], erecv.at[h, dst], e_ss.at[h, k], e_rs.at[h, k], (at_p(k), ex)
        )

    for h in chunks:
        for c in loads[h]:
            c.wait()
        if h == CHUNKS - 1:
            for c in wcopies:
                c.start()
        zsend[h] = dot(pick, x_in[h].reshape(8 * TOK, Q), (1, 0)).astype(BF).reshape(EXP, 32, Q)
        if h == 0:
            pl.semaphore_wait(barrier, EXP - 1 + PL - 1)
            each(EXP, lambda k: c_copy(k, ex).start())
        each(EXP, lambda k, h=h: z_copy(h, k, ex).start())
        zrecv[h, ex] = zsend[h, ex]
    crecv[ex] = csend[ex]
    each(EXP, lambda k: c_copy(k, at_z(EXP - k)).wait_recv())

    total = crecv[0]
    for s in range(1, EXP):
        total = total + crecv[s]
    lsend[...] = total
    lrecv[dp] = total
    each(PL, lambda k: l_copy(k, dp).start())

    lane = iota((8, 256), 1)
    src = lane >> 5
    rank = lane & 3
    used = jnp.zeros((8, 256), jnp.int32)
    for s in range(EXP):
        v = jnp.concatenate([crecv[s], crecv[s]], axis=1)
        used = jnp.where(src == s, v, used)
        if s < EXP - 1:
            rank = rank + jnp.where(src > s, v, 0)
    alive = (lane & 3) < used

    each(PL, lambda k: l_copy(k, at_p(PL - k)).wait_recv())
    zero = jnp.zeros((8, 128), jnp.int32)
    before = zero
    col = lane >> 4
    off_l = jnp.zeros((8, 256), jnp.int32)
    len_l = jnp.zeros((8, 256), jnp.int32)
    running = zero
    for i in range(PL):
        v = lrecv[i]
        off_l = jnp.where(col == i, jnp.concatenate([running, running], axis=1), off_l)
        len_l = jnp.where(col == i, jnp.concatenate([v, v], axis=1), len_l)
        before = before + jnp.where(i < dp, v, zero)
        running = running + v
    dealt = rank + jnp.concatenate([before, before], axis=1)
    to = ((dealt & 15) << 4) + (((lane >> 3) & 3) << 2) + (((lane >> 2) & 1) << 1) + (rank >> 4)
    to = jnp.where(alive, to, -1)[0:1, :]
    qmat[...] = jnp.where(iota((256, 256), 0) == to, F32(1.0), F32(0.0)).astype(BF)
    own = ((dp - off_l + 512) & 15) + ((lane & 1) << 4)
    to = (((lane >> 1) & 1) << 6) + (((lane >> 2) & 3) << 4) + ((off_l + own) >> 4)
    to = jnp.where(own < len_l, to, -1)[0:1, :]
    fmat[...] = jnp.where(iota((128, 256), 0) == to, F32(1.0), F32(0.0)).astype(BF)

    for h in chunks:
        each(EXP, lambda k, h=h: z_copy(h, k, at_z(EXP - k)).wait_recv())
        xsend[h] = (
            dot(qmat[...], zrecv[h].reshape(256, Q), (1, 0)).astype(BF).reshape(PL, ROWS, Q)
        )
        each(PL, lambda k, h=h: x_copy(h, k, dp).start())
        xrecv[h, dp] = xsend[h, dp]

    def compact(h):
        each(PL, lambda k: x_copy(h, k, at_p(PL - k)).wait_recv())
        mine = dot(fmat[...], xrecv[h].reshape(256, Q), (1, 0)).astype(BF)
        for q in range(4):
            tbuf[h, dp, :, pl.ds(q * Q, Q)] = mine[q * 16 : q * 16 + 16]
            sbuf[h, dp, :, pl.ds(q * Q, Q)] = mine[64 + q * 16 : 64 + q * 16 + 16]

    ups = [[lax.rem(v + o, SIDE) if o else v for o in range(SIDE)] for v in (x, y)]
    blocks = [[ups[1][oy] * SIDE + ups[0][ox] for ox in range(SIDE)] for oy in range(SIDE)]

    def block_of(part, ou, ov):
        ou, ov = ou % SIDE, ov % SIDE
        return blocks[ov][ou] if part == 0 else blocks[ou][ov]

    def device(part, du, dv):
        return (block_of(part, du, dv), ex)

    gathered = (tbuf, sbuf)
    sign = (1, -1)
    both = [(part, d) for part in range(2) for d in range(2)]
    sent = []

    def go(c):
        c.start()
        sent.append(c)

    def ag_steps(h):
        def ag(part, ident, block, half, du, dv):
            ref = gathered[part].at[h, block]
            if half is not None:
                ref = ref.at[:, pl.ds(half * H, H)]
            return remote(
                ref, ref, ag_ss.at[h, part, ident], ag_rs.at[h, part, ident], device(part, du, dv)
            )

        def phase2(part, o):
            for d in range(2):
                go(ag(part, 4 + o * 4 + d, block_of(part, o, 0), None, 0, sign[d]))

        def begin():
            for part, d in both:
                go(ag(part, d, block_of(part, 0, 0), None, sign[d], 0))
            for part in range(2):
                phase2(part, 0)

        def near():
            for part, d in both:
                o = 3 if d == 0 else 1
                b = block_of(part, o, 0)
                ag(part, d, b, None, sign[d], 0).wait_recv()
                go(ag(part, 2 + d, b, d, sign[d], 0))
            for part, d in both:
                phase2(part, 3 if d == 0 else 1)

        def far():
            for part, d in both:
                ag(part, 2 + d, block_of(part, 2, 0), d, sign[d], 0).wait_recv()
            for part in range(2):
                phase2(part, 2)

        def pass_on(o):
            for part, d in both:
                b = block_of(part, o, -sign[d])
                ag(part, 4 + o * 4 + d, b, None, 0, sign[d]).wait_recv()
                go(ag(part, 4 + o * 4 + 2 + d, b, d, 0, sign[d]))

        def finish():
            for o in (0, 3, 1, 2):
                for part, d in both:
                    b = block_of(part, o, 2)
                    ag(part, 4 + o * 4 + 2 + d, b, d, 0, sign[d]).wait_recv()

        return begin, near, far, pass_on, finish

    outs = [
        [
            pltpu.make_async_copy(buf.at[h], out.at[h], out_sem.at[h, i])
            for i, (buf, out) in enumerate(((tbuf, t_out), (sbuf, s_out)))
        ]
        for h in chunks
    ]

    def first(buf, w, h):
        return dot(buf[h].reshape(LIVE, W), w[:, pl.ds(h * W, W)], (1, 1))

    def gather_steps(h):
        begin, near, far, pass_on, finish = ag_steps(h)

        def start():
            compact(h)
            begin()

        def end():
            finish()
            for c in outs[h]:
                c.start()
            if h == 0:
                for c in wcopies:
                    c.wait()

        def add(acc, buf, w):
            acc[...] = first(buf, w, h) if h == 0 else acc[...] + first(buf, w, h)

        return [
            start,
            near,
            lambda: pass_on(0),
            far,
            lambda: pass_on(3),
            lambda: pass_on(1),
            lambda: pass_on(2),
            end,
            lambda: add(gate_acc, tbuf, wg),
            lambda: add(up_acc, tbuf, wu),
            lambda: add(grad_acc, sbuf, wd) if h < CHUNKS - 1 else None,
        ]

    interleave([gather_steps(h) for h in chunks], AG_LAG, False)
    pre_gate = gate_acc[...]
    pre_up = up_acc[...]
    sig = jax.nn.sigmoid(pre_gate)
    swish = pre_gate * sig
    hid[...] = (swish * pre_up).astype(BF)
    gate_acc[...] = swish
    up_acc[...] = pre_up * (sig * (1.0 + pre_gate * (1.0 - sig)))

    def hidden_grads():
        hidden_grad = grad_acc[...] + first(sbuf, wd, CHUNKS - 1)
        pgg[...] = (hidden_grad * up_acc[...]).astype(BF)
        pug[...] = (hidden_grad * gate_acc[...]).astype(BF)

    partial = (po, pr)
    shape = (SIDE, SIDE, ROWS, TILE)

    def second(h, part, half):
        def step(n, _):
            cols = pl.ds(pl.multiple_of(h * W + n * TILE, TILE), TILE)
            to = pl.ds(pl.multiple_of(n * TILE, TILE), TILE)
            if part == 0:
                sums = dot(hid[...], wd[:, cols], (1, 0))
            else:
                sums = dot(pgg[...], wg[:, cols], (1, 0)) + dot(pug[...], wu[:, cols], (1, 0))
            partial[part][h, :, :, :, to] = sums.astype(BF).reshape(shape)
            return 0

        lax.fori_loop(half * H // TILE, (half + 1) * H // TILE, step, 0)

    def cols_of(half):
        return pl.ds(half * H, H)

    def rs_steps(h):
        def group(part, ov):
            v = ups[1 - part][ov % SIDE]
            return partial[part].at[h, v] if part == 0 else partial[part].at[h, :, v]

        def piece(part, ou):
            u, v = ups[part][ou % SIDE], ups[1 - part][0]
            return partial[part].at[h, v, u] if part == 0 else partial[part].at[h, u, v]

        def rs(part, ident, src, dst, du, dv):
            return remote(
                src, dst, rs_ss.at[h, part, ident], rs_rs.at[h, part, ident], device(part, du, dv)
            )

        def far(part, d):
            src = group(part, 2).at[:, :, cols_of(d)]
            return rs(part, d, src, r1.at[h, part, d], 0, sign[d])

        def near(part, d, c):
            src = group(part, sign[d]).at[:, :, cols_of(c)]
            return rs(part, 2 + 2 * d + c, src, r2.at[h, part, d, c], 0, sign[d])

        def far_block(part):
            src = piece(part, 2)
            return rs(part, 6, src, r3.at[h, part], 2, 0)

        def near_block(part, d):
            src = piece(part, sign[d])
            return rs(part, 7 + d, src, r4.at[h, part, d], sign[d], 0)

        def begin(part):
            for c in range(2):
                second(h, part, c)
                go(far(part, c))
                go(near(part, 1 - c, c))

        def add_far():
            for d in range(2):
                for part in range(2):
                    far(part, d).wait_recv()
                    ref = group(part, sign[d]).at[:, :, cols_of(d)]
                    ref[...] = (ref[...].astype(F32) + r1[h, part, d].astype(F32)).astype(BF)
                    go(near(part, d, d))

        def add_near():
            for part in range(2):
                for d in range(2):
                    for c in range(2):
                        near(part, d, c).wait_recv()
                for o in (2, 1, 3, 0):
                    u = ups[part][o]
                    for c in range(2):
                        ref = piece(part, o).at[:, cols_of(c)]
                        ref[...] = (
                            ref[...].astype(F32)
                            + r2[h, part, 0, c, u].astype(F32)
                            + r2[h, part, 1, c, u].astype(F32)
                        ).astype(BF)
                    if o == 2:
                        go(far_block(part))
                    elif o != 0:
                        go(near_block(part, 0 if o == 1 else 1))

        def finish():
            reduced = []
            for part in range(2):
                for d in range(2):
                    near_block(part, d).wait_recv()
                far_block(part).wait_recv()
                for q in range(4):
                    cols = pl.ds(q * Q, Q)
                    reduced.append(
                        (
                            piece(part, 0)[:, cols].astype(F32)
                            + r4[h, part, 0, :, cols].astype(F32)
                            + r4[h, part, 1, :, cols].astype(F32)
                            + r3[h, part, :, cols].astype(F32)
                        ).astype(BF)
                    )
            back = dot(fmat[...], jnp.concatenate(reduced, axis=0), (0, 0))
            esend[h] = back.astype(BF).reshape(PL, ROWS, Q)
            each(PL, lambda k: e_copy(h, k, dp).start())
            erecv[h, dp] = esend[h, dp]

        return begin, add_far, add_near, finish

    def to_shards(h):
        each(PL, lambda k: e_copy(h, k, at_p(PL - k)).wait_recv())
        back = dot(qmat[...], erecv[h].reshape(256, Q), (0, 0))
        zsback[h] = back.astype(BF).reshape(EXP, 32, Q)
        each(EXP, lambda k: b_copy(h, k, ex).start())
        keep(h).start()

    def at_shard(h):
        each(EXP, lambda k: b_copy(h, k, at_z(EXP - k)).wait_recv())
        keep(h).wait()

    acts = []

    def turn():
        for i, (src, dst) in enumerate(((hid, hid_t), (pgg, pgg_t), (pug, pug_t))):
            turned[i] = src[...].T
            acts.append(pltpu.make_async_copy(turned.at[i], dst, act_sem.at[i]))
            acts[i].start()

    def reduce_steps(h):
        begin, add_far, add_near, finish = rs_steps(h)

        def start():
            begin(0)
            if h == 0:
                hidden_grads()
            begin(1)
        def middle():
            add_far()
            if h == CHUNKS - 1:
                turn()

        return [
            start,
            middle,
            add_near,
            finish,
            lambda: to_shards(h),
            lambda: at_shard(h),
        ]

    interleave([reduce_steps(h) for h in chunks], RS_LAG, True)

    each(EXP, lambda k: c_copy(k, ex).wait_send())
    each(PL, lambda k: l_copy(k, dp).wait_send())
    for h in chunks:
        each(EXP, lambda k, h=h: z_copy(h, k, ex).wait_send())
        each(EXP, lambda k, h=h: b_copy(h, k, ex).wait_send())
        each(PL, lambda k, h=h: x_copy(h, k, dp).wait_send())
        each(PL, lambda k, h=h: e_copy(h, k, dp).wait_send())
    for c in sent:
        c.wait_send()
    for h in chunks:
        for c in outs[h]:
            c.wait()
    for c in acts:
        c.wait()


def run_main(chosen, gate, counts, tokens, cotangent, wg, wu, wd):
    vmem = pl.BlockSpec(memory_space=pltpu.VMEM)
    anym = pl.BlockSpec(memory_space=pl.ANY)
    dma = pltpu.SemaphoreType.DMA

    def exchange(peers):
        return [pltpu.VMEM((CHUNKS, peers, 256 // peers, Q), BF)] * 2

    return pl.pallas_call(
        main_kernel,
        out_shape=(
            jax.ShapeDtypeStruct((CHUNKS, PL, ROWS, W), BF),
            jax.ShapeDtypeStruct((CHUNKS, PL, ROWS, W), BF),
            jax.ShapeDtypeStruct((HID, LIVE), BF),
            jax.ShapeDtypeStruct((HID, LIVE), BF),
            jax.ShapeDtypeStruct((HID, LIVE), BF),
            jax.ShapeDtypeStruct((CHUNKS, EXP, 32, Q), BF),
        ),
        in_specs=[vmem] * 3 + [pl.BlockSpec(memory_space=pltpu.SMEM)] + [anym] * 5,
        out_specs=(anym,) * 6,
        scratch_shapes=[
            pltpu.VMEM((CHUNKS, 8, TOK, Q), BF),
            *[pltpu.VMEM((HID, D), BF)] * 3,
            pltpu.VMEM((EXP, 8, 128), jnp.int32),
            pltpu.VMEM((EXP, 8, 128), jnp.int32),
            pltpu.VMEM((8, 128), jnp.int32),
            pltpu.VMEM((PL, 8, 128), jnp.int32),
            *exchange(EXP),
            *exchange(PL),
            *exchange(PL),
            exchange(EXP)[0],
            *[pltpu.VMEM((CHUNKS, PL, ROWS, W), BF)] * 2,
            *[pltpu.VMEM((LIVE, HID), F32)] * 3,
            *[pltpu.VMEM((LIVE, HID), BF)] * 3,
            pltpu.VMEM((3, HID, LIVE), BF),
            *[pltpu.VMEM((CHUNKS, SIDE, SIDE, ROWS, W), BF)] * 2,
            pltpu.VMEM((CHUNKS, 2, 2, SIDE, ROWS, H), BF),
            pltpu.VMEM((CHUNKS, 2, 2, 2, SIDE, ROWS, H), BF),
            pltpu.VMEM((CHUNKS, 2, ROWS, W), BF),
            pltpu.VMEM((CHUNKS, 2, 2, ROWS, W), BF),
            pltpu.VMEM((256, 256), BF),
            pltpu.VMEM((128, 256), BF),
            dma((CHUNKS, 8)),
            dma((3,)),
            dma((CHUNKS, 2)),
            dma((3,)),
            dma((CHUNKS,)),
            *[dma((EXP,))] * 2,
            *[dma((PL,))] * 2,
            *[dma((CHUNKS, EXP))] * 2,
            *[dma((CHUNKS, PL))] * 2,
            *[dma((CHUNKS, PL))] * 2,
            *[dma((CHUNKS, EXP))] * 2,
            *[dma((CHUNKS, 2, 20))] * 2,
            *[dma((CHUNKS, 2, 9))] * 2,
        ],
        compiler_params=pltpu.CompilerParams(
            collective_id=0, has_side_effects=True, vmem_limit_bytes=58 * 1024 * 1024
        ),
        cost_estimate=pl.CostEstimate(
            flops=6 * 2 * LIVE * D * HID, bytes_accessed=20 << 20, transcendentals=LIVE * HID
        ),
        name="routed_experts",
    )(chosen, gate, counts, counts, tokens, cotangent, wg, wu, wd)


def tail_kernel(
    chosen_ref, gate_ref, cnt_ref, t_hbm, s_hbm, hid_hbm, pgg_hbm, pug_hbm, zr_hbm, cot_hbm,
    comb_out, tg_out, prob_ref, gg_out, gu_out, gd_out,
    t, s, hid, pgg, pug, zr, cot, comb, tg, gg, gu, gd, in_sem, out_sem,
):
    def load(src, dst, i):
        c = pltpu.make_async_copy(src, dst, in_sem.at[i])
        c.start()
        return c

    order = [
        [load(pgg_hbm, pgg, 0), load(t_hbm.at[0], t.at[0], 1), load(pug_hbm, pug, 2)],
        [load(hid_hbm, hid, 3), load(s_hbm.at[0], s.at[0], 4)],
        [load(zr_hbm, zr, 5), load(cot_hbm, cot, 6)],
    ]
    later = [
        [load(t_hbm.at[h], t.at[h], 5 + 2 * h), load(s_hbm.at[h], s.at[h], 6 + 2 * h)]
        for h in range(1, CHUNKS)
    ]
    stores = []

    def store(src, dst, cols, i, n):
        c = pltpu.make_async_copy(src.at[:, cols], dst.at[:, cols], out_sem.at[i, n])
        c.start()
        stores.append(c)

    r = iota((32, EXP), 0)
    token, weight, used = of_rows(r & 7, r >> 3, chosen_ref, gate_ref, cnt_ref)
    match = iota((32, TOK), 1) == token
    pick_w = jnp.where(match, weight, F32(0.0)).astype(BF)
    pick_live = jnp.where(match, used, F32(0.0)).astype(BF)
    r = iota((64, 1), 0)
    target = ((r & 7) << 5) + ((r >> 5) << 2) + ((r >> 3) & 3)
    lane = iota((64, 256), 1)
    part = jnp.zeros((32, 128), F32)

    def wait(copies):
        for c in copies:
            c.wait()

    for n in range(D // TILE):
        h, at = n * TILE // W, n * TILE % W
        cols = pl.ds(n * TILE, TILE)
        here = pl.ds(at, TILE)
        if n == 0:
            wait(order[0])
        elif at == 0:
            wait(later[h - 1])
        tile = t[h, :, :, here].reshape(LIVE, TILE)
        gg[:, cols] = dot(pgg[...], tile, (1, 0)).astype(BF)
        store(gg, gg_out, cols, 0, n)
        gu[:, cols] = dot(pug[...], tile, (1, 0)).astype(BF)
        store(gu, gu_out, cols, 1, n)
        if n == 0:
            wait(order[1])
        gd[:, cols] = dot(hid[...], s[h, :, :, here].reshape(LIVE, TILE), (1, 0)).astype(BF)
        store(gd, gd_out, cols, 2, n)
        if n == 0:
            wait(order[2])
        pieces = []
        for q in range(at // Q, (at + TILE) // Q):
            pick = jnp.where(lane == target + q * 8, F32(1.0), F32(0.0)).astype(BF)
            pieces.append(dot(pick, zr[h], (1, 0)))
        rows = jnp.concatenate(pieces, axis=1) if len(pieces) > 1 else pieces[0]
        out_rows = rows[:32]
        comb[:, cols] = dot(pick_w, out_rows.astype(BF), (0, 0)).astype(BF)
        store(comb, comb_out, cols, 3, n)
        tg[:, cols] = dot(pick_live, rows[32:].astype(BF), (0, 0)).astype(BF)
        store(tg, tg_out, cols, 4, n)
        prod = dot(pick_live, cot[:, cols], (1, 0)) * out_rows
        for i in range(TILE // 128):
            part = part + prod[:, i * 128 : (i + 1) * 128]

    inner = jnp.sum(part, axis=1, keepdims=True)
    eye = iota((EXP, EXP), 0) == iota((EXP, EXP), 1)
    lines = [
        jnp.sum(jnp.where(eye, inner[m * EXP : (m + 1) * EXP], F32(0.0)), axis=0, keepdims=True)
        for m in range(M)
    ]
    prob_ref[...] = jnp.concatenate(lines, axis=0).astype(BF)
    wait(stores)


def run_tail(chosen, gate, counts, t, s, hid, pgg, pug, zr, cotangent):
    vmem = pl.BlockSpec(memory_space=pltpu.VMEM)
    anym = pl.BlockSpec(memory_space=pl.ANY)
    tokens = jax.ShapeDtypeStruct((TOK, D), BF)
    grads = jax.ShapeDtypeStruct((HID, D), BF)
    return pl.pallas_call(
        tail_kernel,
        out_shape=(tokens, tokens, jax.ShapeDtypeStruct((M, EXP), BF), grads, grads, grads),
        in_specs=[vmem] * 3 + [anym] * 7,
        out_specs=(anym, anym, vmem, anym, anym, anym),
        scratch_shapes=[
            *[pltpu.VMEM((CHUNKS, PL, ROWS, W), BF)] * 2,
            *[pltpu.VMEM((HID, LIVE), BF)] * 3,
            pltpu.VMEM((CHUNKS, 256, Q), BF),
            *[pltpu.VMEM((TOK, D), BF)] * 3,
            *[pltpu.VMEM((HID, D), BF)] * 3,
            pltpu.SemaphoreType.DMA((5 + 2 * CHUNKS,)),
            pltpu.SemaphoreType.DMA((5, D // TILE)),
        ],
        compiler_params=pltpu.CompilerParams(vmem_limit_bytes=58 * 1024 * 1024),
        cost_estimate=pl.CostEstimate(
            flops=3 * 2 * LIVE * D * HID, bytes_accessed=20 << 20, transcendentals=0
        ),
        name="weight_grads_and_combine",
    )(chosen, gate, counts, t, s, hid, pgg, pug, zr, cotangent)


def per_device(tokens, cotangent, chosen, counts, gate_prob, w_gate, w_up, w_down):
    routes = (chosen[0].T, gate_prob[0].T, counts)
    t, s, hid, pgg, pug, zr = run_main(
        *routes, tokens, cotangent, w_gate[0].T, w_up[0].T, w_down[0]
    )
    combined, token_grad, prob_grad, gg, gu, gd = run_tail(
        *routes, t, s, hid, pgg, pug, zr.reshape(CHUNKS, 256, Q), cotangent
    )
    return combined, token_grad, prob_grad.T[None], gg.T[None], gu.T[None], gd[None]


def solution(mesh):
    tokens = P(("dp", "expert"), None)
    slots = P(("dp", "expert"), None, None)
    specs = (tokens, tokens, slots, tokens, slots)
    weights = (P("expert", None, "dp"), P("expert", None, "dp"), P("expert", "dp", None))
    return jax.shard_map(
        per_device,
        mesh=mesh,
        in_specs=specs + weights,
        out_specs=(tokens, tokens, slots) + weights,
        check_vma=False,
    )
```
